256 devices in a mesh: cols: 8 (over z_lo, core), space: 32 (over y, z_hi, x).
Axes of the slice: x: 4, y: 4, z: 8 (z_hi: 2, z_lo: 4; z = z_hi * 4 + z_lo), core: 2. Of those that a mesh axis runs over, the one named last changes fastest.
Arguments:
- mean_state: float32 [6, 512, 256], P(None, 'space', 'cols'), may hold values from -2 to 2
- covariance: float32 [128, 6, 512, 256], P('cols', None, 'space'), may hold values from -2 to 2
- land_mask: int32 [512, 256], replicated, may hold values 0 or 1
- stations: int32 [4096], P('space'), may hold values from 0 to 131071, as said below
- observed: float32 [4096], P('space'), may hold values from -5 to 5
- obs_weight: float32 [4096], P('space'), may hold values from 0.5 to 4
Outputs:
- mean_analysis: float32 [6, 512, 256], P(None, 'space', 'cols')
- covariance_analysis: float32 [128, 6, 512, 256], P('cols', None, 'space')
The draws below stay inside these ranges and needn't reach their ends.
Inputs may be any that keep to these rules, and one draw needn't show every extreme that they name: Stations b * 128 to (b + 1) * 128 - 1 lie in grid rows b * 16 to (b + 1) * 16 - 1; several stations may share a cell.
All inputs are finite; a program needn't handle non-finite values.
Results may differ from the reference program's by a relative error of at most 0.0053.
Values may be sent and summed in bfloat16 or wider, within the bound.
A program may use at most 64 MiB of HBM per device.

```python
import math
import jax
import jax.numpy as jnp
from jax import lax

ROWS = 16
NY = 256
K = 128
OBS_DEV = 128
ITERS = 4
NX = 512
NOBS = 4096


def draw_stations(key, part):
    blocks = NOBS // OBS_DEV
    local_cells = jax.random.randint(key, (blocks, OBS_DEV), 0, ROWS * NY)
    offset = jnp.arange(blocks, dtype=jnp.int32)[:, None] * (ROWS * NY)
    return (local_cells + offset).reshape(-1).astype(jnp.int32)


def draw_covariance(key, part):
    key_common = jax.random.fold_in(key, 11)
    key_own = jax.random.fold_in(key, 12)
    key_amp = jax.random.fold_in(key, 13)
    common = jax.random.normal(key_common, (6, NX, NY), jnp.float32)
    amplitude = jax.random.uniform(key_amp, (K, 1, 1, 1), jnp.float32, 0.4, 1.0)
    own = jax.random.normal(key_own, (K, 6, NX, NY), jnp.float32)
    values = 0.3 * (0.7 * amplitude * common[None] + 0.7 * own)
    return jnp.clip(values, -2.0, 2.0).astype(jnp.float32)


def place_ends(values, key, smallest, top_value):
    shape = values.shape
    index_at = [jax.random.randint(jax.random.fold_in(key, axis), (), 0, shape[axis]) for axis in range(len(shape))]
    values = values.at[tuple(index_at)].set(smallest)
    longest = shape.index(max(shape))
    index_at[longest] = (index_at[longest] + 1) % shape[longest]
    return values.at[tuple(index_at)].set(top_value)


def shard_levels(key, shape, split, least, top_value):
    def one(dim, blocks):
        steps = jax.random.uniform(jax.random.fold_in(jax.random.fold_in(key, 6), dim), (blocks,), jnp.float32, least / len(split), top_value / len(split))
        return jnp.repeat(jnp.exp(steps), shape[dim] // blocks).reshape((-1,) + (1,) * (len(shape) - dim - 1))

    factor_of = one(*split[0])
    for cut in split[1:]:
        factor_of = factor_of * one(*cut)
    return factor_of


def gaussian(stream_key, shape, width, reach, split=(), held_as=jnp.bfloat16):
    array = jax.random.normal(stream_key, shape, jnp.float32) * width
    if len(split) > 0:
        array = shard_levels(stream_key, shape, split, -0.22, 0.18) * array
    return jnp.clip(array, min=-reach, max=reach).astype(held_as)


def setup_inputs(seed: int = 0) -> dict:
    arg_keys = jax.random.split(jax.random.key(seed), 7)
    return {
        "mean_state": gaussian(arg_keys[0], (6, NX, NY), 0.5, 2.0, ((1, 32), (2, 8)), jnp.float32),
        "covariance": draw_covariance(jax.random.fold_in(arg_keys[6], 71), 0),
        "land_mask": place_ends((jax.random.randint(arg_keys[2], (NX, NY), 0, 10) < 9).astype(jnp.int32), jax.random.fold_in(arg_keys[2], 1), 0, 1),
        "stations": draw_stations(jax.random.fold_in(arg_keys[6], 71), 0),
        "observed": gaussian(arg_keys[4], (NOBS,), 1.0, 5.0, ((0, 32),), jnp.float32),
        "obs_weight": jnp.clip(jnp.exp(math.log(4.0) - 2.0794415 * jax.random.uniform(arg_keys[5], (NOBS,), jnp.float32) ** shard_levels(arg_keys[5], (NOBS,), ((0, 32),), -0.2, 0.2)), 0.5, 4.0),
    }


time_step = 0.5
gravity = 1.0
reduced_gravity = 0.125
coriolis = 0.3
friction = 0.05
layer_depths = (1.0, 2.0)

def diff_rows(values):
    return 0.5 * (values[..., 2:, 1:-1] - values[..., :-2, 1:-1])

def diff_cols(values):
    return 0.5 * (values[..., 1:-1, 2:] - values[..., 1:-1, :-2])

def inner(values):
    return values[..., 1:-1, 1:-1]

def velocities(field, wet_cells):
    wet_inner = inner(wet_cells)
    surface = field[..., 0, :, :] + field[..., 3, :, :]
    pressure_top = gravity * surface
    pressure_pair = (pressure_top, pressure_top - reduced_gravity * field[..., 0, :, :])
    velocity_pairs = []
    for layer_index in range(2):
        zonal = inner(field[..., 3 * layer_index + 1, :, :])
        north = inner(field[..., 3 * layer_index + 2, :, :])
        pressure = pressure_pair[layer_index]
        zonal_new = wet_inner * (zonal + time_step * (-diff_rows(pressure) + coriolis * north - friction * zonal))
        north_new = wet_inner * (north + time_step * (-diff_cols(pressure) - coriolis * zonal - friction * north))
        velocity_pairs.append((zonal_new, north_new))
    return velocity_pairs

def mean_core(padded, wet_cells):
    velocity_pairs = velocities(padded, wet_cells)
    fields = []
    carried = []
    for layer_index in range(2):
        thickness = padded[3 * layer_index]
        column_depth = layer_depths[layer_index] + inner(thickness)
        zonal_new, north_new = velocity_pairs[layer_index]
        updated = thickness[2:-2, 2:-2] - time_step * (diff_rows(column_depth * zonal_new) + diff_cols(column_depth * north_new))
        fields += [updated, zonal_new[1:-1, 1:-1], north_new[1:-1, 1:-1]]
        carried += [thickness[1:-1, 2:-2], zonal_new[:, 1:-1], north_new[:, 1:-1]]
    return (jnp.stack(fields), jnp.stack(carried))

def tangent_core(padded, carried, wet_cells):
    beside_all = jnp.pad(carried, ((0, 0), (0, 0), (1, 1)))
    velocity_pairs = velocities(padded, wet_cells)
    fields = []
    for layer_index in range(2):
        thickness = padded[..., 3 * layer_index, :, :]
        column_depth = layer_depths[layer_index] + beside_all[3 * layer_index]
        zonal_new, north_new = velocity_pairs[layer_index]
        flux_rows = column_depth * zonal_new + inner(thickness) * beside_all[3 * layer_index + 1]
        flux_cols = column_depth * north_new + inner(thickness) * beside_all[3 * layer_index + 2]
        updated = thickness[..., 2:-2, 2:-2] - time_step * (diff_rows(flux_rows) + diff_cols(flux_cols))
        fields += [updated, zonal_new[..., 1:-1, 1:-1], north_new[..., 1:-1, 1:-1]]
    return jnp.stack(fields, axis=-3)

def reference(mean_state, covariance, land_mask, stations, observed, obs_weight):
    wet_all = jnp.pad(land_mask.astype(jnp.float32), 2)
    mean_now = mean_state
    columns = covariance
    for step_index in range(ITERS):
        mean_next, carried = mean_core(jnp.pad(mean_now, ((0, 0), (2, 2), (2, 2))), wet_all)

        def advance(column_block):
            return tangent_core(jnp.pad(column_block, ((0, 0), (0, 0), (2, 2), (2, 2))), carried, wet_all)
        blocks = columns.reshape((8, K // 8) + columns.shape[1:])
        columns = lax.map(advance, blocks).reshape(columns.shape)
        mean_now = mean_next
    surface = (mean_now[0] + mean_now[3]).reshape(-1)
    innovation = obs_weight * (observed - surface[stations])
    column_surface = (columns[:, 0] + columns[:, 3]).reshape(K, -1)
    sensed = column_surface[:, stations] * obs_weight[None, :]
    identity = jnp.eye(K, dtype=jnp.float32)
    gram_matrix = identity + jnp.dot(sensed.astype(jnp.float32), sensed.T.astype(jnp.float32), precision=lax.Precision.HIGHEST, preferred_element_type=jnp.float32)
    target = jnp.dot(sensed.astype(jnp.float32), innovation.astype(jnp.float32), precision=lax.Precision.HIGHEST, preferred_element_type=jnp.float32)
    lower_factor = lax.linalg.cholesky(gram_matrix)
    halfway = lax.linalg.triangular_solve(lower_factor, target[:, None], left_side=True, lower=True)
    weights = lax.linalg.triangular_solve(lower_factor, halfway, left_side=True, lower=True, transpose_a=True)[:, 0]
    inverse = lax.linalg.triangular_solve(lower_factor, identity, left_side=True, lower=True)
    transform = inverse.T
    increment = jnp.einsum('k,kfxy->fxy', weights, columns, precision=lax.Precision.HIGHEST)
    mean_analysis = mean_now + increment
    transform_low = transform.astype(jnp.bfloat16)
    columns_low = columns.astype(jnp.bfloat16).reshape(K, -1)
    updated = jnp.dot(transform_low.T.astype(jnp.float32), columns_low.astype(jnp.float32), preferred_element_type=jnp.float32)
    return (mean_analysis, updated.reshape(columns.shape))
```

```python
import functools

import jax
import jax.numpy as jnp
from jax import lax
from jax.experimental import pallas as pl
from jax.experimental.pallas import tpu as pltpu
from jax.sharding import PartitionSpec as P

STEPS = 4
HALO = 8
TILE = 16
WIN = TILE + 2 * HALO
NC = 8
NS = 32
NCOL = 16
KALL = 128
WIDTH = 256
FR = 96
PIECE = 12
OBS = 128

HIGH = lax.Precision.HIGHEST
MESH = pl.DeviceIdType.MESH
ANY = pl.BlockSpec(memory_space=pl.ANY)
VMEM = pl.BlockSpec(memory_space=pltpu.VMEM)


def peer(c, s):
    return {"cols": c, "space": s}


def greet(peers):
    barrier = pltpu.get_barrier_semaphore()
    for device in peers:
        pl.semaphore_signal(barrier, inc=1, device_id=device, device_id_type=MESH)
    pl.semaphore_wait(barrier, len(peers))


def remote(src, dst, send, recv, device):
    return pltpu.make_async_remote_copy(
        src_ref=src, dst_ref=dst, send_sem=send, recv_sem=recv, device_id=device, device_id_type=MESH
    )


def halo_kernel(
    top_ref, bottom_ref, piece_ref, above_ref, below_ref, mean_ref, halo_send, halo_recv, mean_send, mean_recv, own_sem
):
    c = lax.axis_index("cols")
    s = lax.axis_index("space")
    down, up = lax.rem(s + 1, NS), lax.rem(s + NS - 1, NS)
    others = [lax.rem(c + i, NC) for i in range(1, NC)]
    targets = [(o, s, 1) for o in others]
    for o in [c] + others:
        targets += [(o, down, 0), (o, up, 2)]
    greet([peer(o, t) for o, t, _ in targets])
    own = pltpu.make_async_copy(piece_ref, mean_ref.at[1, c], own_sem)
    own.start()
    to_down = remote(bottom_ref, above_ref, halo_send.at[0], halo_recv.at[0], peer(c, down))
    to_up = remote(top_ref, below_ref, halo_send.at[1], halo_recv.at[1], peer(c, up))
    copies = []
    for i, (o, t, slot) in enumerate(targets):
        copies.append(
            remote(piece_ref, mean_ref.at[slot, c], mean_send.at[i], mean_recv.at[slot, c], peer(o, t))
        )
        copies[-1].start()
    to_down.start()
    to_up.start()
    for slot in range(3):
        for o in others if slot == 1 else [c] + others:
            remote(
                piece_ref, mean_ref.at[slot, o], mean_send.at[0], mean_recv.at[slot, o], peer(o, down)
            ).wait_recv()
    for copy in copies:
        copy.wait_send()
    own.wait()
    to_down.wait()
    to_up.wait()


def halo_exchange(top, bottom, piece):
    return pl.pallas_call(
        halo_kernel,
        out_shape=(
            jax.ShapeDtypeStruct(bottom.shape, bottom.dtype),
            jax.ShapeDtypeStruct(top.shape, top.dtype),
            jax.ShapeDtypeStruct((3, NC) + piece.shape, piece.dtype),
        ),
        in_specs=[ANY] * 3,
        out_specs=(ANY,) * 3,
        scratch_shapes=[
            pltpu.SemaphoreType.DMA((2,)),
            pltpu.SemaphoreType.DMA((2,)),
            pltpu.SemaphoreType.DMA((3 * NC - 1,)),
            pltpu.SemaphoreType.DMA((3, NC)),
            pltpu.SemaphoreType.DMA,
        ],
        compiler_params=pltpu.CompilerParams(collective_id=0, has_side_effects=True),
        name="halo_exchange",
    )(top, bottom, piece)


def row_difference(a):
    rows = a.shape[0]
    return pltpu.roll(a, rows - 1, 0) - pltpu.roll(a, 1, 0)


def col_difference(a, first, last):
    width = a.shape[1]
    after = jnp.where(last, 0.0, pltpu.roll(a, width - 1, 1))
    before = jnp.where(first, 0.0, pltpu.roll(a, 1, 1))
    return after - before


def new_velocities(fields, wet, first, last):
    top_pressure = fields[0] + fields[3]
    pressures = (top_pressure, top_pressure - 0.125 * fields[0])
    pairs = []
    for layer in range(2):
        u, v = fields[3 * layer + 1], fields[3 * layer + 2]
        p = pressures[layer]
        u_new = wet * (0.975 * u + 0.15 * v - 0.25 * row_difference(p))
        v_new = wet * (0.975 * v - 0.15 * u - 0.25 * col_difference(p, first, last))
        pairs.append((u_new, v_new))
    return pairs


def forecast_kernel(
    cov_ref,
    above_ref,
    below_ref,
    mean_ref,
    wet_ref,
    inside_ref,
    row_ref,
    col_ref,
    weight_ref,
    observed_ref,
    columns_ref,
    sensed_ref,
    meanf_ref,
    carried,
    held,
    surface,
    per_step,
):
    grid_step = pl.program_id(0)
    lane = lax.broadcasted_iota(jnp.int32, (WIN, WIDTH), 1)
    first, last = lane == 0, lane == WIDTH - 1
    wet = wet_ref[...]
    inside = inside_ref[...]

    @pl.when(grid_step == 0)
    def _():
        fields = [mean_ref[f] * inside for f in range(6)]
        for step in range(STEPS):
            pairs = new_velocities(fields, wet, first, last)
            after = []
            for layer in range(2):
                h = fields[3 * layer]
                depth = (1.0, 2.0)[layer] + h
                u, v = pairs[layer]
                base = 6 * step + 3 * layer
                carried[base] = depth
                carried[base + 1] = u
                carried[base + 2] = v
                h_new = inside * (h - 0.25 * (row_difference(depth * u) + col_difference(depth * v, first, last)))
                after += [h_new, u, v]
            fields = after
        for f in range(6):
            meanf_ref[pl.ds(TILE * f, TILE)] = fields[f][HALO : HALO + TILE]
        surface[pl.ds(NCOL * TILE, TILE)] = (fields[0] + fields[3])[HALO : HALO + TILE]

    for i in range(per_step):
        k = grid_step * per_step + i
        above = above_ref[i].astype(jnp.float32)
        below = below_ref[i].astype(jnp.float32)
        fields = []
        for f in range(6):
            rows = jnp.concatenate(
                [
                    above[HALO * f : HALO * (f + 1)],
                    cov_ref[i, pl.ds(TILE * f, TILE)],
                    below[HALO * f : HALO * (f + 1)],
                ],
                axis=0,
            )
            fields.append(rows * inside)
        for step in range(STEPS):
            pairs = new_velocities(fields, wet, first, last)
            after = []
            for layer in range(2):
                h = fields[3 * layer]
                u, v = pairs[layer]
                base = 6 * step + 3 * layer
                depth = carried[base]
                rows_flux = depth * u + h * carried[base + 1]
                cols_flux = depth * v + h * carried[base + 2]
                h_new = inside * (h - 0.25 * (row_difference(rows_flux) + col_difference(cols_flux, first, last)))
                after += [h_new, u, v]
            fields = after
        for f in range(6):
            at = pl.ds(pl.multiple_of(k * FR + TILE * f, TILE), TILE)
            for half in range(2):
                held[half, at] = fields[f][HALO : HALO + TILE, 128 * half : 128 * (half + 1)]
        surface[pl.ds(pl.multiple_of(k * TILE, TILE), TILE)] = (fields[0] + fields[3])[HALO : HALO + TILE]

    @pl.when(grid_step == pl.num_programs(0) - 1)
    def _():
        cells = lax.broadcasted_iota(jnp.int32, (WIDTH, OBS), 0)
        pick = (cells == col_ref[...]).astype(jnp.float32)
        at_rows = lax.broadcasted_iota(jnp.int32, (TILE, OBS), 0) == row_ref[...]
        picked = jnp.dot(surface[...], pick, precision=HIGH, preferred_element_type=jnp.float32)
        picked = picked.reshape(NCOL + 1, TILE, OBS)
        values = jnp.sum(jnp.where(at_rows[None], picked, 0.0), axis=1)
        weight = weight_ref[...]
        sensed_ref[pl.ds(0, NCOL)] = values[:NCOL] * weight
        innovation = weight * (observed_ref[...] - values[NCOL:])
        below_first = lax.broadcasted_iota(jnp.int32, (8, OBS), 0) > 0
        sensed_ref[pl.ds(NCOL, 8)] = jnp.where(below_first, 0.0, jnp.broadcast_to(innovation, (8, OBS)))

        def gather_row(fr, carry):
            for half in range(2):
                value = held[half, pl.ds(fr, NCOL, stride=FR)]
                columns_ref[fr, :, 128 * half : 128 * (half + 1)] = value.astype(jnp.bfloat16)
            return carry

        lax.fori_loop(0, FR, gather_row, 0, unroll=8)


def forecast(cov, above, below, mean, wet, inside, row, col, weight, observed):
    per_step = 2
    block = lambda rows: pl.BlockSpec((per_step, rows, WIDTH), lambda i: (i, 0, 0))
    whole = lambda shape: pl.BlockSpec(shape, lambda i: (0,) * len(shape))
    return pl.pallas_call(
        functools.partial(forecast_kernel, per_step=per_step),
        grid=(NCOL // per_step,),
        out_shape=(
            jax.ShapeDtypeStruct((FR, NCOL, WIDTH), jnp.bfloat16),
            jax.ShapeDtypeStruct((NCOL + 8, OBS), jnp.float32),
            jax.ShapeDtypeStruct((FR, WIDTH), jnp.float32),
        ),
        in_specs=[
            block(FR),
            block(6 * HALO),
            block(6 * HALO),
            whole((6, WIN, WIDTH)),
            whole((WIN, WIDTH)),
            whole((WIN, WIDTH)),
            whole((1, OBS)),
            whole((1, OBS)),
            whole((1, OBS)),
            whole((1, OBS)),
        ],
        out_specs=(whole((FR, NCOL, WIDTH)), whole((NCOL + 8, OBS)), whole((FR, WIDTH))),
        scratch_shapes=[
            pltpu.VMEM((6 * STEPS, WIN, WIDTH), jnp.float32),
            pltpu.VMEM((2, NCOL * FR, 128), jnp.float32),
            pltpu.VMEM(((NCOL + 1) * TILE, WIDTH), jnp.float32),
        ],
        compiler_params=pltpu.CompilerParams(vmem_limit_bytes=40 * 1024 * 1024),
        name="forecast",
    )(cov, above, below, mean, wet, inside, row, col, weight, observed)


def gram_kernel(
    columns_ref, sensed_ref, cells_ref, gram_ref, right, block, across, layers,
    send_a, recv_a, send_b, recv_b, send_c, recv_c, send_d, recv_d, own_sem,
):
    c = lax.axis_index("cols")
    s = lax.axis_index("space")
    y, zh, x = s // 8, lax.rem(s // 4, 2), lax.rem(s, 4)
    plane = y * 4 + x
    others = [lax.rem(c + i, NC) for i in range(1, NC)]
    planes = [lax.rem(plane + i, 16) for i in range(1, 16)]
    space_of = lambda p: (p // 4) * 8 + zh * 4 + lax.rem(p, 4)
    far = y * 8 + (1 - zh) * 4 + x
    line = [(o, s, zh * NC + o) for o in others] + [(o, far, (1 - zh) * NC + o) for o in [c] + others]
    greet([peer(o, t) for o, t, _ in line] + [peer(c, space_of(p)) for p in planes])

    own_rows = pl.ds(pl.multiple_of(c * NCOL, NCOL), NCOL)
    mine = sensed_ref.at[pl.ds(0, NCOL)]
    first = []
    for i, o in enumerate(others):
        copy = remote(mine, right.at[own_rows], send_a.at[i], recv_a.at[c], peer(o, s))
        copy.start()
        first.append(copy)
    bulk = []
    for i, o in enumerate(others):
        source = columns_ref.at[pl.ds(o * PIECE, PIECE)]
        copy = remote(source, cells_ref.at[:, own_rows], send_d.at[i], recv_d.at[c], peer(o, s))
        copy.start()
        bulk.append(copy)
    own = pltpu.make_async_copy(columns_ref.at[pl.ds(c * PIECE, PIECE)], cells_ref.at[:, own_rows], own_sem)
    own.start()

    right[own_rows] = sensed_ref[pl.ds(0, NCOL)]
    right[pl.ds(KALL, 8)] = sensed_ref[pl.ds(NCOL, 8)]
    right[pl.ds(KALL + 8, KALL - 8)] = jnp.zeros((KALL - 8, OBS), jnp.float32)
    for o in others:
        rows = pl.ds(pl.multiple_of(o * NCOL, NCOL), NCOL)
        remote(mine, right.at[rows], send_a.at[0], recv_a.at[o], peer(o, s)).wait_recv()
    part = lax.dot_general(
        sensed_ref[pl.ds(0, NCOL)], right[...], (((1,), (1,)), ((), ())),
        precision=HIGH, preferred_element_type=jnp.float32,
    )
    block[...] = part
    second = []
    for i, p in enumerate(planes):
        copy = remote(block, across.at[plane], send_b.at[i], recv_b.at[plane], peer(c, space_of(p)))
        copy.start()
        second.append(copy)
    across[plane] = part
    for p in planes:
        remote(block, across.at[p], send_b.at[0], recv_b.at[p], peer(c, space_of(p))).wait_recv()
    total = across[0]
    for p in range(1, 16):
        total = total + across[p]
    place = zh * NC + c
    layers[place] = total
    third = []
    for i, (o, t, _) in enumerate(line):
        copy = remote(layers.at[place], layers.at[place], send_c.at[i], recv_c.at[place], peer(o, t))
        copy.start()
        third.append(copy)
    for o, t, slot in line:
        remote(layers.at[slot], layers.at[slot], send_c.at[0], recv_c.at[slot], peer(o, t)).wait_recv()
    for o in range(NC):
        gram_ref[pl.ds(o * NCOL, NCOL)] = layers[o] + layers[NC + o]
    for o in others:
        rows = pl.ds(pl.multiple_of(o * NCOL, NCOL), NCOL)
        source = columns_ref.at[pl.ds(0, PIECE)]
        remote(source, cells_ref.at[:, rows], send_d.at[0], recv_d.at[o], peer(o, s)).wait_recv()
    own.wait()
    for copy in first + second + third + bulk:
        copy.wait_send()


def gram_exchange(columns, sensed):
    dma = pltpu.SemaphoreType.DMA
    return pl.pallas_call(
        gram_kernel,
        out_shape=(
            jax.ShapeDtypeStruct((PIECE, KALL, WIDTH), jnp.bfloat16),
            jax.ShapeDtypeStruct((KALL, 2 * KALL), jnp.float32),
        ),
        in_specs=[ANY, VMEM],
        out_specs=(ANY, VMEM),
        scratch_shapes=[
            pltpu.VMEM((2 * KALL, OBS), jnp.float32),
            pltpu.VMEM((NCOL, 2 * KALL), jnp.float32),
            pltpu.VMEM((16, NCOL, 2 * KALL), jnp.float32),
            pltpu.VMEM((2 * NC, NCOL, 2 * KALL), jnp.float32),
            dma((NC - 1,)),
            dma((NC,)),
            dma((15,)),
            dma((16,)),
            dma((15,)),
            dma((16,)),
            dma((NC - 1,)),
            dma((NC,)),
            dma,
        ],
        compiler_params=pltpu.CompilerParams(collective_id=1, has_side_effects=True),
        name="gram_exchange",
    )(columns, sensed)


def transform_kernel(
    transform_ref, weights_ref, cells_ref, result_ref, increment_ref, made, added,
    send_a, recv_a, send_b, recv_b, own_sems,
):
    c = lax.axis_index("cols")
    s = lax.axis_index("space")
    others = [lax.rem(c + i, NC) for i in range(1, NC)]
    greet([peer(o, s) for o in others])
    transform = transform_ref[...]
    weights = weights_ref[...]
    for fr in range(PIECE):
        cell = cells_ref[fr]
        out = jnp.dot(transform, cell, preferred_element_type=jnp.float32)
        made[fr] = out.astype(jnp.bfloat16)
        row = jnp.dot(weights, cell.astype(jnp.float32), precision=HIGH, preferred_element_type=jnp.float32)
        added[fr] = row
    copies = []
    mine = pl.ds(c * PIECE, PIECE)
    for i, o in enumerate(others):
        rows = pl.ds(pl.multiple_of(o * NCOL, NCOL), NCOL)
        copies.append(
            remote(made.at[:, rows], result_ref.at[mine], send_a.at[i], recv_a.at[c], peer(o, s))
        )
        copies.append(remote(added, increment_ref.at[c], send_b.at[i], recv_b.at[c], peer(o, s)))
    for copy in copies:
        copy.start()
    own_rows = pl.ds(pl.multiple_of(c * NCOL, NCOL), NCOL)
    own = pltpu.make_async_copy(made.at[:, own_rows], result_ref.at[mine], own_sems.at[0])
    own_added = pltpu.make_async_copy(added, increment_ref.at[c], own_sems.at[1])
    own.start()
    own_added.start()
    for o in others:
        theirs = result_ref.at[pl.ds(o * PIECE, PIECE)]
        remote(made.at[:, own_rows], theirs, send_a.at[0], recv_a.at[o], peer(o, s)).wait_recv()
        remote(added, increment_ref.at[o], send_b.at[0], recv_b.at[o], peer(o, s)).wait_recv()
    own.wait()
    own_added.wait()
    for copy in copies:
        copy.wait_send()


def transform_exchange(transform, weights, cells):
    dma = pltpu.SemaphoreType.DMA
    return pl.pallas_call(
        transform_kernel,
        out_shape=(
            jax.ShapeDtypeStruct((FR, NCOL, WIDTH), jnp.bfloat16),
            jax.ShapeDtypeStruct((NC, PIECE, 8, WIDTH), jnp.float32),
        ),
        in_specs=[VMEM] * 3,
        out_specs=(ANY, ANY),
        scratch_shapes=[
            pltpu.VMEM((PIECE, KALL, WIDTH), jnp.bfloat16),
            pltpu.VMEM((PIECE, 8, WIDTH), jnp.float32),
            dma((NC - 1,)),
            dma((NC,)),
            dma((NC - 1,)),
            dma((NC,)),
            dma((2,)),
        ],
        compiler_params=pltpu.CompilerParams(collective_id=2, has_side_effects=True),
        name="transform_exchange",
    )(transform, weights, cells)


def place_kernel(result_ref, out_ref, wide):
    for half in range(2):
        part = result_ref[:, :, 128 * half : 128 * (half + 1)].astype(jnp.float32)
        wide[half] = part.reshape(8 * NCOL, 128)
    for j in range(NCOL):
        for half in range(2):
            out_ref[j, :, 128 * half : 128 * (half + 1)] = wide[half, pl.ds(j, 8, stride=NCOL)]


def place(result):
    return pl.pallas_call(
        place_kernel,
        grid=(FR // 8,),
        out_shape=jax.ShapeDtypeStruct((NCOL, FR, WIDTH), jnp.float32),
        in_specs=[pl.BlockSpec((8, NCOL, WIDTH), lambda i: (i, 0, 0))],
        out_specs=pl.BlockSpec((NCOL, 8, WIDTH), lambda i: (0, i, 0)),
        scratch_shapes=[pltpu.VMEM((2, 8 * NCOL, 128), jnp.float32)],
        name="place",
    )(result)


def mean_windows(gathered):
    wide = gathered.reshape(3, NC, 6, TILE, WIDTH // NC).transpose(2, 0, 3, 1, 4).reshape(6, 3, TILE, WIDTH)
    return jnp.concatenate([wide[:, 0, TILE - HALO :], wide[:, 1], wide[:, 2, :HALO]], axis=1)


def local(mean_state, covariance, land_mask, stations, observed, obs_weight):
    s = lax.axis_index("space")
    c = lax.axis_index("cols")
    first_row = s * TILE
    top = covariance[:, :, :HALO].astype(jnp.bfloat16).reshape(NCOL, 6 * HALO, WIDTH)
    bottom = covariance[:, :, TILE - HALO :].astype(jnp.bfloat16).reshape(NCOL, 6 * HALO, WIDTH)
    piece = mean_state.reshape(-1, 128)
    above, below, gathered = halo_exchange(top, bottom, piece)
    pad = ((HALO, HALO), (0, 0))
    wet = lax.dynamic_slice_in_dim(jnp.pad(land_mask, pad), first_row, WIN, 0).astype(jnp.float32)
    grid_row = first_row - HALO + lax.broadcasted_iota(jnp.int32, (WIN, WIDTH), 0)
    inside = ((grid_row >= 0) & (grid_row < NS * TILE)).astype(jnp.float32)
    cell = stations - first_row * WIDTH
    columns, sensed, mean_forecast = forecast(
        covariance.reshape(NCOL, FR, WIDTH),
        above,
        below,
        mean_windows(gathered),
        wet,
        inside,
        (cell // WIDTH)[None],
        (cell % WIDTH)[None],
        obs_weight[None],
        observed[None],
    )
    cells, gram = gram_exchange(columns, sensed)
    identity = jnp.eye(KALL, dtype=jnp.float32)
    lower = lax.linalg.cholesky(identity + gram[:, :KALL])
    inverse = lax.linalg.triangular_solve(lower, identity, left_side=True, lower=True)
    halfway = jnp.dot(inverse, gram[:, KALL], precision=HIGH)
    weights = jnp.dot(halfway, inverse, precision=HIGH)
    result, increments = transform_exchange(
        inverse.astype(jnp.bfloat16), jnp.broadcast_to(weights[None], (8, KALL)), cells
    )
    updated = place(result).reshape(NCOL, 6, TILE, WIDTH)
    increment = increments[:, :, 0].reshape(FR, WIDTH)
    mean = (mean_forecast + increment).reshape(6, TILE, WIDTH)
    width = WIDTH // NC
    return lax.dynamic_slice_in_dim(mean, c * width, width, 2), updated


def solution(mesh):
    return jax.shard_map(
        local,
        mesh=mesh,
        in_specs=(
            P(None, "space", "cols"),
            P("cols", None, "space", None),
            P(),
            P("space"),
            P("space"),
            P("space"),
        ),
        out_specs=(P(None, "space", "cols"), P("cols", None, "space", None)),
        check_vma=False,
    )
```

```python
import jax
import jax.numpy as jnp
from jax import lax
from jax.experimental import pallas as pl
from jax.experimental.pallas import tpu as pltpu
from jax.sharding import PartitionSpec as P

STEPS = 4
HALO = 8
TILE = 16
WIN = TILE + 2 * HALO
NC = 8
NS = 32
NCOL = 16
KALL = 128
WIDTH = 256
FR = 96
PIECE = 12
OBS = 128

HIGH = lax.Precision.HIGHEST
MESH = pl.DeviceIdType.MESH
ANY = pl.BlockSpec(memory_space=pl.ANY)
VMEM = pl.BlockSpec(memory_space=pltpu.VMEM)


def peer(c, s):
    return {"cols": c, "space": s}


def greet(peers):
    barrier = pltpu.get_barrier_semaphore()
    for device in peers:
        pl.semaphore_signal(barrier, inc=1, device_id=device, device_id_type=MESH)
    pl.semaphore_wait(barrier, len(peers))


def remote(src, dst, send, recv, device):
    return pltpu.make_async_remote_copy(
        src_ref=src, dst_ref=dst, send_sem=send, recv_sem=recv, device_id=device, device_id_type=MESH
    )


def row_difference(a):
    rows = a.shape[0]
    return pltpu.roll(a, rows - 1, 0) - pltpu.roll(a, 1, 0)


def col_difference(a, first, last):
    width = a.shape[1]
    after = jnp.where(last, 0.0, pltpu.roll(a, width - 1, 1))
    before = jnp.where(first, 0.0, pltpu.roll(a, 1, 1))
    return after - before


def new_velocities(fields, wet, first, last):
    top_pressure = fields[0] + fields[3]
    pressures = (top_pressure, top_pressure - 0.125 * fields[0])
    pairs = []
    for layer in range(2):
        u, v = fields[3 * layer + 1], fields[3 * layer + 2]
        p = pressures[layer]
        u_new = wet * (0.975 * u + 0.15 * v - 0.25 * row_difference(p))
        v_new = wet * (0.975 * v - 0.15 * u - 0.25 * col_difference(p, first, last))
        pairs.append((u_new, v_new))
    return pairs


BLOCK = 32


def factor(gram, stack):
    stack[...] = jnp.zeros(stack.shape, jnp.float32)
    row = lax.broadcasted_iota(jnp.int32, (BLOCK, KALL), 0)
    lane = lax.broadcasted_iota(jnp.int32, (BLOCK, KALL), 1)

    def one(b, carry):
        start = pl.multiple_of(b * BLOCK, BLOCK)
        back = lax.rem(KALL - start, KALL)
        done = stack[...]
        turned = pltpu.roll(done[:, :KALL], back, 1)
        product = lax.dot_general(
            turned, done, (((0,), (0,)), ((), ())), precision=HIGH, preferred_element_type=jnp.float32
        )[:BLOCK]
        eye = (lane == row + start).astype(jnp.float32)
        left = gram[pl.ds(start, BLOCK)] + eye - product[:, :KALL]
        right = eye - product[:, KALL:]
        square = pltpu.roll(left, back, 1)
        cols = [jnp.broadcast_to(square[:, m : m + 1], (BLOCK, KALL)) for m in range(BLOCK)]
        scale = jnp.zeros((BLOCK, KALL), jnp.float32)
        for j in range(BLOCK):
            r = lax.rsqrt(cols[j][j : j + 1])
            col = cols[j] * r
            strict = jnp.where(row > j, col, 0.0)
            for m in range(j + 1, BLOCK):
                cols[m] = cols[m] - strict * col[m : m + 1]
            left = left - strict * (left[j : j + 1] * r)
            right = right - strict * (right[j : j + 1] * r)
            scale = jnp.where(row == j, r, scale)
        stack[pl.ds(start, BLOCK), :KALL] = left * scale
        stack[pl.ds(start, BLOCK), KALL:] = right * scale
        return carry

    lax.fori_loop(0, KALL // BLOCK, one, 0)


CHUNKS = 8
PER = NCOL // CHUNKS
EDGE = PER * 6 * HALO
GROUPS = 4
GROUP = PIECE // GROUPS


def filter_kernel(
    cov_ref, piece_ref, land_ref, stations_ref, observed_ref, weight_ref,
    result_ref, increment_ref, meanf_ref,
    cov, wet_rows, low, high, above, below, pieces, wide, carried, held, surface, columns, cells,
    sensed, right, block, across, layers, gram, stack, made, added,
    load_sem, small_sem, halo_send, halo_recv, m1_send, m1_recv, m2_send, m2_recv,
    send_a, recv_a, send_b, recv_b, send_c, recv_c, send_d, recv_d, send_e, recv_e, send_f, recv_f, own_sem,
):
    c = lax.axis_index("cols")
    s = lax.axis_index("space")
    down, up = lax.rem(s + 1, NS), lax.rem(s + NS - 1, NS)
    y, zh, x = s // 8, lax.rem(s // 4, 2), lax.rem(s, 4)
    plane = y * 4 + x
    others = [lax.rem(c + i, NC) for i in range(1, NC)]
    planes = [lax.rem(plane + i, 16) for i in range(1, 16)]
    space_of = lambda p: (p // 4) * 8 + zh * 4 + lax.rem(p, 4)
    far = y * 8 + (1 - zh) * 4 + x
    line = [(o, s, zh * NC + o) for o in others] + [(o, far, (1 - zh) * NC + o) for o in [c] + others]

    peers = [peer(c, down), peer(c, up)] + [peer(o, t) for o, t, _ in line] + [peer(c, space_of(p)) for p in planes]
    barrier = pltpu.get_barrier_semaphore()
    for device in peers:
        pl.semaphore_signal(barrier, inc=1, device_id=device, device_id_type=MESH)

    def load(i):
        at = pl.ds(pl.multiple_of(i * PER, PER), PER)
        return pltpu.make_async_copy(cov_ref.at[at], cov.at[at], load_sem.at[i])

    def start_load(i, carry):
        load(i).start()
        return carry

    lax.fori_loop(0, CHUNKS, start_load, 0)
    top_row = pl.multiple_of(jnp.maximum(s * TILE - HALO, 0), HALO)
    end_row = pl.multiple_of(jnp.minimum(s * TILE + TILE, NS * TILE - HALO), HALO)
    own_row = pl.multiple_of(s * TILE, TILE)
    smalls = [
        pltpu.make_async_copy(land_ref.at[pl.ds(top_row, HALO)], wet_rows.at[pl.ds(0, HALO)], small_sem.at[0]),
        pltpu.make_async_copy(land_ref.at[pl.ds(own_row, TILE)], wet_rows.at[pl.ds(HALO, TILE)], small_sem.at[1]),
        pltpu.make_async_copy(
            land_ref.at[pl.ds(end_row, HALO)], wet_rows.at[pl.ds(HALO + TILE, HALO)], small_sem.at[2]
        ),
    ]
    for copy in smalls:
        copy.start()
    pieces[1, c] = piece_ref[...]

    def convert(i):
        for n in range(PER):
            k = i * PER + n
            rows = pl.ds(n * 6 * HALO, 6 * HALO)
            upper = [cov[k, pl.ds(TILE * f, HALO)] for f in range(6)]
            lower = [cov[k, pl.ds(TILE * f + HALO, HALO)] for f in range(6)]
            low[i, rows] = jnp.concatenate(upper, axis=0).astype(jnp.bfloat16)
            high[i, rows] = jnp.concatenate(lower, axis=0).astype(jnp.bfloat16)

    def to_down(i):
        return remote(high.at[i], above.at[i], halo_send.at[0, i], halo_recv.at[0, i], peer(c, down))

    def to_up(i):
        return remote(low.at[i], below.at[i], halo_send.at[1, i], halo_recv.at[1, i], peer(c, up))

    load(0).wait()
    convert(0)
    pl.semaphore_wait(barrier, len(peers))
    phase = [
        remote(piece_ref, pieces.at[0, c], m1_send.at[0], m1_recv.at[0], peer(c, down)),
        remote(piece_ref, pieces.at[2, c], m1_send.at[1], m1_recv.at[1], peer(c, up)),
    ]
    for copy in phase:
        copy.start()
    to_down(0).start()
    to_up(0).start()

    def send_halo(i, carry):
        load(i).wait()
        convert(i)
        to_down(i).start()
        to_up(i).start()
        return carry

    lax.fori_loop(1, CHUNKS, send_halo, 0)
    for copy in phase:
        copy.wait()
    shared = []
    for i, o in enumerate(others):
        copy = remote(pieces.at[:, c], pieces.at[:, c], m2_send.at[i], m2_recv.at[c], peer(o, s))
        copy.start()
        shared.append(copy)

    lane = lax.broadcasted_iota(jnp.int32, (WIN, WIDTH), 1)
    first, last = lane == 0, lane == WIDTH - 1
    grid_row = s * TILE - HALO + lax.broadcasted_iota(jnp.int32, (WIN, WIDTH), 0)
    inside = ((grid_row >= 0) & (grid_row < NS * TILE)).astype(jnp.float32)
    for copy in smalls:
        copy.wait()
    wet = wet_rows[...].astype(jnp.float32) * inside
    for o in others:
        remote(pieces.at[:, o], pieces.at[:, o], m2_send.at[0], m2_recv.at[o], peer(o, s)).wait_recv()
    quarter = lax.broadcasted_iota(jnp.int32, (24, 128), 1) // 32
    for slot in range(3):
        for half in range(2):
            for q in range(4):
                rows = jnp.zeros((24, 128), jnp.float32)
                for p in range(4):
                    value = pieces[slot, 4 * half + p]
                    value = pltpu.roll(value, (32 * (p - q)) % 128, 1) if p != q else value
                    rows = jnp.where(quarter == p, value, rows)
                wide[slot, pl.ds(24 * q, 24), 128 * half : 128 * (half + 1)] = rows
    fields = []
    for f in range(6):
        rows = [
            wide[0, pl.ds(TILE * f + HALO, HALO)],
            wide[1, pl.ds(TILE * f, TILE)],
            wide[2, pl.ds(TILE * f, HALO)],
        ]
        fields.append(jnp.concatenate(rows, axis=0) * inside)
    for step in range(STEPS):
        pairs = new_velocities(fields, wet, first, last)
        after = []
        for layer in range(2):
            h = fields[3 * layer]
            depth = (1.0, 2.0)[layer] + h
            u, v = pairs[layer]
            base = 6 * step + 3 * layer
            carried[base] = depth
            carried[base + 1] = u
            carried[base + 2] = v
            h_new = inside * (h - 0.25 * (row_difference(depth * u) + col_difference(depth * v, first, last)))
            after += [h_new, u, v]
        fields = after
    for f in range(6):
        meanf_ref[pl.ds(TILE * f, TILE)] = fields[f][HALO : HALO + TILE]
    surface[pl.ds(NCOL * TILE, TILE)] = (fields[0] + fields[3])[HALO : HALO + TILE]

    def advance(i, carry):
        to_down(i).wait_recv()
        to_up(i).wait_recv()
        for n in range(PER):
            k = i * PER + n
            rows = pl.ds(n * 6 * HALO, 6 * HALO)
            before = above[i, rows].astype(jnp.float32)
            behind = below[i, rows].astype(jnp.float32)
            fields = []
            for f in range(6):
                parts = [
                    before[HALO * f : HALO * (f + 1)],
                    cov[k, pl.ds(TILE * f, TILE)],
                    behind[HALO * f : HALO * (f + 1)],
                ]
                fields.append(jnp.concatenate(parts, axis=0) * inside)
            for step in range(STEPS):
                pairs = new_velocities(fields, wet, first, last)
                after = []
                for layer in range(2):
                    h = fields[3 * layer]
                    u, v = pairs[layer]
                    base = 6 * step + 3 * layer
                    depth = carried[base]
                    rows_flux = depth * u + h * carried[base + 1]
                    cols_flux = depth * v + h * carried[base + 2]
                    change = row_difference(rows_flux) + col_difference(cols_flux, first, last)
                    after += [inside * (h - 0.25 * change), u, v]
                fields = after
            for f in range(6):
                at = pl.ds(pl.multiple_of(k * FR + TILE * f, TILE), TILE)
                for half in range(2):
                    held[half, at] = fields[f][HALO : HALO + TILE, 128 * half : 128 * (half + 1)]
            surface[pl.ds(pl.multiple_of(k * TILE, TILE), TILE)] = (fields[0] + fields[3])[HALO : HALO + TILE]
        return carry

    lax.fori_loop(0, CHUNKS, advance, 0)

    cell = stations_ref[...] - s * (TILE * WIDTH)
    pick = (lax.broadcasted_iota(jnp.int32, (WIDTH, OBS), 0) == cell % WIDTH).astype(jnp.float32)
    at_rows = lax.broadcasted_iota(jnp.int32, (TILE, OBS), 0) == cell // WIDTH
    picked = jnp.dot(surface[...], pick, precision=HIGH, preferred_element_type=jnp.float32)
    picked = picked.reshape(NCOL + 1, TILE, OBS)
    values = jnp.sum(jnp.where(at_rows[None], picked, 0.0), axis=1)
    weight = weight_ref[...]
    mine = values[:NCOL] * weight
    innovation = weight * (observed_ref[...] - values[NCOL:])
    below_first = lax.broadcasted_iota(jnp.int32, (8, OBS), 0) > 0
    sensed[pl.ds(0, NCOL)] = mine
    sensed[pl.ds(NCOL, 8)] = jnp.where(below_first, 0.0, jnp.broadcast_to(innovation, (8, OBS)))
    own_rows = pl.ds(pl.multiple_of(c * NCOL, NCOL), NCOL)
    rows_of = lambda o: pl.ds(pl.multiple_of(o * NCOL, NCOL), NCOL)
    sent = []
    for i, o in enumerate(others):
        copy = remote(sensed.at[pl.ds(0, NCOL)], right.at[own_rows], send_a.at[i], recv_a.at[c], peer(o, s))
        copy.start()
        sent.append(copy)
    right[own_rows] = mine

    def gather_row(fr, carry):
        for half in range(2):
            value = held[half, pl.ds(fr, NCOL, stride=FR)]
            columns[fr, :, 128 * half : 128 * (half + 1)] = value.astype(jnp.bfloat16)
        return carry

    lax.fori_loop(0, FR, gather_row, 0, unroll=8)
    for i, o in enumerate(others):
        source = columns.at[pl.ds(o * PIECE, PIECE)]
        copy = remote(source, cells.at[:, own_rows], send_d.at[i], recv_d.at[c], peer(o, s))
        copy.start()
        sent.append(copy)
    own_cells = pltpu.make_async_copy(columns.at[pl.ds(c * PIECE, PIECE)], cells.at[:, own_rows], own_sem.at[0])
    own_cells.start()

    for o in others:
        source = sensed.at[pl.ds(0, NCOL)]
        remote(source, right.at[rows_of(o)], send_a.at[0], recv_a.at[o], peer(o, s)).wait_recv()
    part = lax.dot_general(
        sensed[...], right[...], (((1,), (1,)), ((), ())), precision=HIGH, preferred_element_type=jnp.float32
    )
    block[...] = part
    for i, p in enumerate(planes):
        copy = remote(block, across.at[plane], send_b.at[i], recv_b.at[plane], peer(c, space_of(p)))
        copy.start()
        sent.append(copy)
    across[plane] = part
    for p in planes:
        remote(block, across.at[p], send_b.at[0], recv_b.at[p], peer(c, space_of(p))).wait_recv()
    total = across[0]
    for p in range(1, 16):
        total = total + across[p]
    place_ = zh * NC + c
    layers[place_] = total
    for i, (o, t, _) in enumerate(line):
        copy = remote(layers.at[place_], layers.at[place_], send_c.at[i], recv_c.at[place_], peer(o, t))
        copy.start()
        sent.append(copy)
    for o, t, slot in line:
        remote(layers.at[slot], layers.at[slot], send_c.at[0], recv_c.at[slot], peer(o, t)).wait_recv()
    for o in range(NC):
        gram[pl.ds(o * NCOL, NCOL)] = layers[o, pl.ds(0, NCOL)] + layers[NC + o, pl.ds(0, NCOL)]
    target = layers[0, pl.ds(NCOL, 8)][:1] + layers[NC, pl.ds(NCOL, 8)][:1]
    factor(gram, stack)
    inverse = stack[:, KALL:]
    halfway = jnp.sum(inverse * target, axis=1, keepdims=True)
    weights = jnp.sum(halfway * inverse, axis=0, keepdims=True)
    w_hi = weights.astype(jnp.bfloat16).astype(jnp.float32)
    w_mid = (weights - w_hi).astype(jnp.bfloat16).astype(jnp.float32)
    w_low = weights - w_hi - w_mid
    row16 = lax.broadcasted_iota(jnp.int32, (NCOL, KALL), 0)
    extra = jnp.where(row16 == 0, w_hi, jnp.where(row16 == 1, w_mid, jnp.where(row16 == 2, w_low, 0.0)))
    transform = jnp.concatenate([inverse.astype(jnp.bfloat16), extra.astype(jnp.bfloat16)], axis=0)

    for o in others:
        source = columns.at[pl.ds(0, PIECE)]
        remote(source, cells.at[:, rows_of(o)], send_d.at[0], recv_d.at[o], peer(o, s)).wait_recv()
    own_cells.wait()
    for g in range(GROUPS):
        for fr in range(g * GROUP, (g + 1) * GROUP):
            out = jnp.dot(transform, cells[fr], preferred_element_type=jnp.float32)
            made[fr] = out[:KALL].astype(jnp.bfloat16)
            added[pl.ds(fr, 1)] = out[KALL : KALL + 1] + out[KALL + 1 : KALL + 2] + out[KALL + 2 : KALL + 3]
        some = pl.ds(g * GROUP, GROUP)
        goal = pl.ds(c * PIECE + g * GROUP, GROUP)
        for i, o in enumerate(others):
            copy = remote(
                made.at[some, rows_of(o)], result_ref.at[goal], send_e.at[g, i], recv_e.at[g, c], peer(o, s)
            )
            copy.start()
            sent.append(copy)
    for i, o in enumerate(others):
        copy = remote(added, increment_ref.at[c], send_f.at[i], recv_f.at[c], peer(o, s))
        copy.start()
        sent.append(copy)
    own_made = pltpu.make_async_copy(
        made.at[:, own_rows], result_ref.at[pl.ds(c * PIECE, PIECE)], own_sem.at[0]
    )
    own_made.start()
    increment_ref[c] = added[...]
    for o in others:
        for g in range(GROUPS):
            theirs = result_ref.at[pl.ds(o * PIECE + g * GROUP, GROUP)]
            some = pl.ds(g * GROUP, GROUP)
            remote(made.at[some, own_rows], theirs, send_e.at[0, 0], recv_e.at[g, o], peer(o, s)).wait_recv()
        remote(added, increment_ref.at[o], send_f.at[0], recv_f.at[o], peer(o, s)).wait_recv()
    own_made.wait()
    for copy in sent + shared:
        copy.wait_send()

    def wait_halo(i, carry):
        to_down(i).wait_send()
        to_up(i).wait_send()
        return carry

    lax.fori_loop(0, CHUNKS, wait_halo, 0)


def filter_step(cov, piece, land, stations, observed, weight):
    dma = pltpu.SemaphoreType.DMA
    f32, bf16 = jnp.float32, jnp.bfloat16
    return pl.pallas_call(
        filter_kernel,
        out_shape=(
            jax.ShapeDtypeStruct((FR, NCOL, WIDTH), bf16),
            jax.ShapeDtypeStruct((NC, NCOL, WIDTH), f32),
            jax.ShapeDtypeStruct((FR, WIDTH), f32),
        ),
        in_specs=[ANY, VMEM, ANY, VMEM, VMEM, VMEM],
        out_specs=(VMEM, VMEM, VMEM),
        scratch_shapes=[
            pltpu.VMEM((NCOL, FR, WIDTH), f32),
            pltpu.VMEM((WIN, WIDTH), jnp.int32),
            pltpu.VMEM((CHUNKS, EDGE, WIDTH), bf16),
            pltpu.VMEM((CHUNKS, EDGE, WIDTH), bf16),
            pltpu.VMEM((CHUNKS, EDGE, WIDTH), bf16),
            pltpu.VMEM((CHUNKS, EDGE, WIDTH), bf16),
            pltpu.VMEM((3, NC, 24, 128), f32),
            pltpu.VMEM((3, FR, WIDTH), f32),
            pltpu.VMEM((6 * STEPS, WIN, WIDTH), f32),
            pltpu.VMEM((2, NCOL * FR, 128), f32),
            pltpu.VMEM(((NCOL + 1) * TILE, WIDTH), f32),
            pltpu.VMEM((FR, NCOL, WIDTH), bf16),
            pltpu.VMEM((PIECE, KALL, WIDTH), bf16),
            pltpu.VMEM((NCOL + 8, OBS), f32),
            pltpu.VMEM((KALL, OBS), f32),
            pltpu.VMEM((NCOL + 8, KALL), f32),
            pltpu.VMEM((16, NCOL + 8, KALL), f32),
            pltpu.VMEM((2 * NC, NCOL + 8, KALL), f32),
            pltpu.VMEM((KALL, KALL), f32),
            pltpu.VMEM((KALL, 2 * KALL), f32),
            pltpu.VMEM((PIECE, KALL, WIDTH), bf16),
            pltpu.VMEM((NCOL, WIDTH), f32),
            dma((CHUNKS,)),
            dma((3,)),
            dma((2, CHUNKS)),
            dma((2, CHUNKS)),
            dma((2,)),
            dma((2,)),
            dma((NC - 1,)),
            dma((NC,)),
            dma((NC - 1,)),
            dma((NC,)),
            dma((15,)),
            dma((16,)),
            dma((15,)),
            dma((16,)),
            dma((NC - 1,)),
            dma((NC,)),
            dma((GROUPS, NC - 1)),
            dma((GROUPS, NC)),
            dma((NC - 1,)),
            dma((NC,)),
            dma((1,)),
        ],
        compiler_params=pltpu.CompilerParams(
            collective_id=0, has_side_effects=True, vmem_limit_bytes=48 * 1024 * 1024
        ),
        name="filter_step",
    )(cov, piece, land, stations, observed, weight)


PAIR = 2


def place_kernel(result_ref, increment_ref, meanf_ref, out_ref, mean_ref, held, total):
    j = pl.program_id(0)

    @pl.when(j == 0)
    def _():
        for half in range(2):
            part = result_ref[:, :, 128 * half : 128 * (half + 1)].astype(jnp.float32)
            held[half] = part.reshape(FR * NCOL, 128)
        for o in range(NC):
            rows = pl.ds(o * PIECE, PIECE)
            total[rows] = meanf_ref[rows] + increment_ref[o][:PIECE]
        c = lax.axis_index("cols")
        width = WIDTH // NC
        turned = pltpu.roll(total[...], lax.rem(WIDTH - c * width, WIDTH), 1)
        mean_ref[...] = turned[:, :width]

    for n in range(PAIR):
        for half in range(2):
            out_ref[n, :, 128 * half : 128 * (half + 1)] = held[half, pl.ds(j * PAIR + n, FR, stride=NCOL)]


def place(result, increment, mean_forecast):
    whole = lambda shape: pl.BlockSpec(shape, lambda i: (0,) * len(shape))
    return pl.pallas_call(
        place_kernel,
        grid=(NCOL // PAIR,),
        out_shape=(
            jax.ShapeDtypeStruct((NCOL, FR, WIDTH), jnp.float32),
            jax.ShapeDtypeStruct((FR, WIDTH // NC), jnp.float32),
        ),
        in_specs=[whole((FR, NCOL, WIDTH)), whole((NC, NCOL, WIDTH)), whole((FR, WIDTH))],
        out_specs=(pl.BlockSpec((PAIR, FR, WIDTH), lambda i: (i, 0, 0)), whole((FR, WIDTH // NC))),
        scratch_shapes=[pltpu.VMEM((2, FR * NCOL, 128), jnp.float32), pltpu.VMEM((FR, WIDTH), jnp.float32)],
        compiler_params=pltpu.CompilerParams(vmem_limit_bytes=24 * 1024 * 1024),
        name="place",
    )(result, increment, mean_forecast)


def local(mean_state, covariance, land_mask, stations, observed, obs_weight):
    piece = mean_state.reshape(4, 24, WIDTH // NC).transpose(1, 0, 2).reshape(24, 128)
    result, increment, mean_forecast = filter_step(
        covariance.reshape(NCOL, FR, WIDTH), piece, land_mask, stations[None], observed[None], obs_weight[None]
    )
    updated, mean = place(result, increment, mean_forecast)
    return mean.reshape(mean_state.shape), updated.reshape(covariance.shape)


def solution(mesh):
    return jax.shard_map(
        local,
        mesh=mesh,
        in_specs=(
            P(None, "space", "cols"),
            P("cols", None, "space", None),
            P(),
            P("space"),
            P("space"),
            P("space"),
        ),
        out_specs=(P(None, "space", "cols"), P("cols", None, "space", None)),
        check_vma=False,
    )
```

```python
import jax
import jax.numpy as jnp
from jax import lax
from jax.experimental import pallas as pl
from jax.experimental.pallas import tpu as pltpu
from jax.sharding import PartitionSpec as P

STEPS = 4
HALO = 8
TILE = 16
WIN = TILE + 2 * HALO
NC = 8
NS = 32
NCOL = 16
KALL = 128
WIDTH = 256
FR = 96
PIECE = 12
OBS = 128

HIGH = lax.Precision.HIGHEST
MESH = pl.DeviceIdType.MESH
ANY = pl.BlockSpec(memory_space=pl.ANY)
VMEM = pl.BlockSpec(memory_space=pltpu.VMEM)
HBM = pl.BlockSpec(memory_space=pltpu.HBM)


def peer(c, s):
    return {"cols": c, "space": s}


def greet(peers):
    barrier = pltpu.get_barrier_semaphore()
    for device in peers:
        pl.semaphore_signal(barrier, inc=1, device_id=device, device_id_type=MESH)
    pl.semaphore_wait(barrier, len(peers))


def remote(src, dst, send, recv, device):
    return pltpu.make_async_remote_copy(
        src_ref=src, dst_ref=dst, send_sem=send, recv_sem=recv, device_id=device, device_id_type=MESH
    )


def row_difference(a):
    rows = a.shape[0]
    return pltpu.roll(a, rows - 1, 0) - pltpu.roll(a, 1, 0)


def col_difference(a, first, last):
    width = a.shape[1]
    after = jnp.where(last, 0.0, pltpu.roll(a, width - 1, 1))
    before = jnp.where(first, 0.0, pltpu.roll(a, 1, 1))
    return after - before


def new_velocities(fields, wet, first, last):
    top_pressure = fields[0] + fields[3]
    pressures = (top_pressure, top_pressure - 0.125 * fields[0])
    pairs = []
    for layer in range(2):
        u, v = fields[3 * layer + 1], fields[3 * layer + 2]
        p = pressures[layer]
        u_new = wet * (0.975 * u + 0.15 * v - 0.25 * row_difference(p))
        v_new = wet * (0.975 * v - 0.15 * u - 0.25 * col_difference(p, first, last))
        pairs.append((u_new, v_new))
    return pairs


BLOCK = 32


def factor(gram, stack):
    stack[...] = jnp.zeros(stack.shape, jnp.float32)
    row = lax.broadcasted_iota(jnp.int32, (BLOCK, KALL), 0)
    lane = lax.broadcasted_iota(jnp.int32, (BLOCK, KALL), 1)

    def one(b, carry):
        start = pl.multiple_of(b * BLOCK, BLOCK)
        back = lax.rem(KALL - start, KALL)
        done = stack[...]
        turned = pltpu.roll(done[:, :KALL], back, 1)
        product = lax.dot_general(
            turned, done, (((0,), (0,)), ((), ())), precision=HIGH, preferred_element_type=jnp.float32
        )[:BLOCK]
        eye = (lane == row + start).astype(jnp.float32)
        left = gram[pl.ds(start, BLOCK)] + eye - product[:, :KALL]
        right = eye - product[:, KALL:]
        square = pltpu.roll(left, back, 1)
        cols = [jnp.broadcast_to(square[:, m : m + 1], (BLOCK, KALL)) for m in range(BLOCK)]
        scale = jnp.zeros((BLOCK, KALL), jnp.float32)
        for j in range(BLOCK):
            r = lax.rsqrt(cols[j][j : j + 1])
            col = cols[j] * r
            strict = jnp.where(row > j, col, 0.0)
            for m in range(j + 1, BLOCK):
                cols[m] = cols[m] - strict * col[m : m + 1]
            left = left - strict * (left[j : j + 1] * r)
            right = right - strict * (right[j : j + 1] * r)
            scale = jnp.where(row == j, r, scale)
        stack[pl.ds(start, BLOCK), :KALL] = left * scale
        stack[pl.ds(start, BLOCK), KALL:] = right * scale
        return carry

    lax.fori_loop(0, KALL // BLOCK, one, 0)


CHUNKS = 8
AHEAD = 4
PER = NCOL // CHUNKS
EDGE = PER * 6 * HALO
GROUPS = 4
GROUP = PIECE // GROUPS


def filter_kernel(
    cov_ref, piece_ref, land_ref, stations_hbm, observed_hbm, weight_hbm,
    result_ref, increment_ref, meanf_ref,
    cov, wet_rows, stations_ref, observed_ref, weight_ref, low, high, above, below, pieces, wide, carried, held, surface, columns, cells,
    sensed, right, block, across, layers, gram, stack, made, added,
    load_sem, small_sem, halo_send, halo_recv, m1_send, m1_recv, m2_send, m2_recv,
    send_a, recv_a, send_b, recv_b, send_c, recv_c, send_d, recv_d, send_e, recv_e, send_f, recv_f, own_sem,
):
    c = lax.axis_index("cols")
    s = lax.axis_index("space")
    down, up = lax.rem(s + 1, NS), lax.rem(s + NS - 1, NS)
    y, zh, x = s // 8, lax.rem(s // 4, 2), lax.rem(s, 4)
    plane = y * 4 + x
    others = [lax.rem(c + i, NC) for i in range(1, NC)]
    planes = [lax.rem(plane + i, 16) for i in range(1, 16)]
    space_of = lambda p: (p // 4) * 8 + zh * 4 + lax.rem(p, 4)
    far = y * 8 + (1 - zh) * 4 + x
    chip, core = c // 2, lax.rem(c, 2)
    partner = 2 * chip + 1 - core
    chips = [lax.rem(chip + i, 4) for i in range(1, 4)]
    line = [(q, s, zh) for q in chips] + [(q, far, 1 - zh) for q in [chip] + chips]
    same_core = lambda q: 2 * q + core

    peers = [peer(c, down), peer(c, up)] + [peer(o, s) for o in others]
    peers += [peer(same_core(q), far) for q in [chip] + chips] + [peer(c, space_of(p)) for p in planes]
    barrier = pltpu.get_barrier_semaphore()
    for device in peers:
        pl.semaphore_signal(barrier, inc=1, device_id=device, device_id_type=MESH)

    def load(i):
        at = pl.ds(pl.multiple_of(i * PER, PER), PER)
        return pltpu.make_async_copy(cov_ref.at[at], cov.at[at], load_sem.at[i])

    def start_load(i, carry):
        load(i).start()
        return carry

    lax.fori_loop(0, CHUNKS, start_load, 0)
    top_row = pl.multiple_of(jnp.maximum(s * TILE - HALO, 0), HALO)
    end_row = pl.multiple_of(jnp.minimum(s * TILE + TILE, NS * TILE - HALO), HALO)
    own_row = pl.multiple_of(s * TILE, TILE)
    smalls = [
        pltpu.make_async_copy(land_ref.at[pl.ds(top_row, HALO)], wet_rows.at[pl.ds(0, HALO)], small_sem.at[0]),
        pltpu.make_async_copy(land_ref.at[pl.ds(own_row, TILE)], wet_rows.at[pl.ds(HALO, TILE)], small_sem.at[1]),
        pltpu.make_async_copy(
            land_ref.at[pl.ds(end_row, HALO)], wet_rows.at[pl.ds(HALO + TILE, HALO)], small_sem.at[2]
        ),
        pltpu.make_async_copy(stations_hbm, stations_ref, small_sem.at[3]),
        pltpu.make_async_copy(observed_hbm, observed_ref, small_sem.at[4]),
        pltpu.make_async_copy(weight_hbm, weight_ref, small_sem.at[5]),
    ]
    for copy in smalls:
        copy.start()
    pieces[core, chip, 1] = piece_ref[0]
    pieces[core, chip, 2] = piece_ref[1]

    def convert(i):
        for n in range(PER):
            k = i * PER + n
            rows = pl.ds(n * 6 * HALO, 6 * HALO)
            upper = [cov[k, pl.ds(TILE * f, HALO)] for f in range(6)]
            lower = [cov[k, pl.ds(TILE * f + HALO, HALO)] for f in range(6)]
            low[i, rows] = jnp.concatenate(upper, axis=0).astype(jnp.bfloat16)
            high[i, rows] = jnp.concatenate(lower, axis=0).astype(jnp.bfloat16)

    def to_down(i):
        return remote(high.at[i], above.at[i], halo_send.at[0, i], halo_recv.at[0, i], peer(c, down))

    def to_up(i):
        return remote(low.at[i], below.at[i], halo_send.at[1, i], halo_recv.at[1, i], peer(c, up))

    load(0).wait()
    convert(0)
    pl.semaphore_wait(barrier, len(peers))
    phase = [
        remote(piece_ref.at[1], pieces.at[core, chip, 0], m1_send.at[0], m1_recv.at[0], peer(c, down)),
        remote(piece_ref.at[0], pieces.at[core, chip, 3], m1_send.at[1], m1_recv.at[1], peer(c, up)),
    ]
    for copy in phase:
        copy.start()
    to_down(0).start()
    to_up(0).start()

    def send_halo(i, carry):
        load(i).wait()
        convert(i)

        @pl.when(i < AHEAD)
        def _():
            to_down(i).start()
            to_up(i).start()

        return carry

    lax.fori_loop(1, CHUNKS, send_halo, 0)
    for copy in phase:
        copy.wait()
    shared = []
    for i, q in enumerate(chips):
        ours = pieces.at[core, chip]
        copy = remote(ours, ours, m2_send.at[i], m2_recv.at[chip], peer(same_core(q), s))
        copy.start()
        shared.append(copy)

    lane = lax.broadcasted_iota(jnp.int32, (WIN, WIDTH), 1)
    first, last = lane == 0, lane == WIDTH - 1
    grid_row = s * TILE - HALO + lax.broadcasted_iota(jnp.int32, (WIN, WIDTH), 0)
    inside = ((grid_row >= 0) & (grid_row < NS * TILE)).astype(jnp.float32)
    for copy in smalls:
        copy.wait()
    wet = wet_rows[...].astype(jnp.float32) * inside
    for q in chips:
        theirs = pieces.at[core, q]
        remote(theirs, theirs, m2_send.at[0], m2_recv.at[q], peer(same_core(q), s)).wait_recv()
    swap = remote(pieces.at[core], pieces.at[core], m2_send.at[3], m2_recv.at[4], peer(partner, s))
    swap.start()
    swap.wait()
    quarter = lax.broadcasted_iota(jnp.int32, (12, 128), 1) // 32
    for slot in range(4):
        for half in range(2):
            for q in range(4):
                rows = jnp.zeros((12, 128), jnp.float32)
                for p in range(4):
                    value = pieces[p % 2, 2 * half + p // 2, slot]
                    value = pltpu.roll(value, (32 * (p - q)) % 128, 1) if p != q else value
                    rows = jnp.where(quarter == p, value, rows)
                wide[slot, pl.ds(12 * q, 12), 128 * half : 128 * (half + 1)] = rows
    fields = []
    for f in range(6):
        rows = [wide[slot, pl.ds(HALO * f, HALO)] for slot in range(4)]
        fields.append(jnp.concatenate(rows, axis=0) * inside)
    for step in range(STEPS):
        pairs = new_velocities(fields, wet, first, last)
        after = []
        for layer in range(2):
            h = fields[3 * layer]
            depth = (1.0, 2.0)[layer] + h
            u, v = pairs[layer]
            base = 6 * step + 3 * layer
            carried[base] = depth
            carried[base + 1] = u
            carried[base + 2] = v
            h_new = inside * (h - 0.25 * (row_difference(depth * u) + col_difference(depth * v, first, last)))
            after += [h_new, u, v]
        fields = after
    for f in range(6):
        meanf_ref[pl.ds(TILE * f, TILE)] = fields[f][HALO : HALO + TILE]
    surface[pl.ds(NCOL * TILE, TILE)] = (fields[0] + fields[3])[HALO : HALO + TILE]

    def advance(i, carry):
        to_down(i).wait_send()
        to_up(i).wait_send()

        @pl.when(i + AHEAD < CHUNKS)
        def _():
            to_down(i + AHEAD).start()
            to_up(i + AHEAD).start()

        to_down(i).wait_recv()
        to_up(i).wait_recv()
        for n in range(PER):
            k = i * PER + n
            rows = pl.ds(n * 6 * HALO, 6 * HALO)
            before = above[i, rows].astype(jnp.float32)
            behind = below[i, rows].astype(jnp.float32)
            fields = []
            for f in range(6):
                parts = [
                    before[HALO * f : HALO * (f + 1)],
                    cov[k, pl.ds(TILE * f, TILE)],
                    behind[HALO * f : HALO * (f + 1)],
                ]
                fields.append(jnp.concatenate(parts, axis=0) * inside)
            for step in range(STEPS):
                pairs = new_velocities(fields, wet, first, last)
                after = []
                for layer in range(2):
                    h = fields[3 * layer]
                    u, v = pairs[layer]
                    base = 6 * step + 3 * layer
                    depth = carried[base]
                    rows_flux = depth * u + h * carried[base + 1]
                    cols_flux = depth * v + h * carried[base + 2]
                    change = row_difference(rows_flux) + col_difference(cols_flux, first, last)
                    after += [inside * (h - 0.25 * change), u, v]
                fields = after
            for f in range(6):
                at = pl.ds(pl.multiple_of(k * FR + TILE * f, TILE), TILE)
                for half in range(2):
                    held[half, at] = fields[f][HALO : HALO + TILE, 128 * half : 128 * (half + 1)]
            surface[pl.ds(pl.multiple_of(k * TILE, TILE), TILE)] = (fields[0] + fields[3])[HALO : HALO + TILE]
        return carry

    lax.fori_loop(0, CHUNKS, advance, 0)

    cell = stations_ref[...] - s * (TILE * WIDTH)
    pick = (lax.broadcasted_iota(jnp.int32, (WIDTH, OBS), 0) == cell % WIDTH).astype(jnp.float32)
    at_rows = lax.broadcasted_iota(jnp.int32, (TILE, OBS), 0) == cell // WIDTH
    picked = jnp.dot(surface[...], pick, precision=HIGH, preferred_element_type=jnp.float32)
    picked = picked.reshape(NCOL + 1, TILE, OBS)
    values = jnp.sum(jnp.where(at_rows[None], picked, 0.0), axis=1)
    weight = weight_ref[...]
    mine = values[:NCOL] * weight
    innovation = weight * (observed_ref[...] - values[NCOL:])
    below_first = lax.broadcasted_iota(jnp.int32, (8, OBS), 0) > 0
    sensed[pl.ds(0, NCOL)] = mine
    sensed[pl.ds(NCOL, 8)] = jnp.where(below_first, 0.0, jnp.broadcast_to(innovation, (8, OBS)))
    own_rows = pl.ds(pl.multiple_of(c * NCOL, NCOL), NCOL)
    rows_of = lambda o: pl.ds(pl.multiple_of(o * NCOL, NCOL), NCOL)
    sent = []
    for i, q in enumerate(chips):
        source = sensed.at[pl.ds(0, NCOL)]
        copy = remote(source, right.at[chip, core], send_a.at[i], recv_a.at[chip], peer(same_core(q), s))
        copy.start()
        sent.append(copy)
    right[chip, core] = mine

    def gather_row(fr, carry):
        for half in range(2):
            value = held[half, pl.ds(fr, NCOL, stride=FR)]
            columns[fr, :, 128 * half : 128 * (half + 1)] = value.astype(jnp.bfloat16)
        return carry

    lax.fori_loop(0, FR, gather_row, 0, unroll=8)
    for i, o in enumerate(others):
        source = columns.at[pl.ds(o * PIECE, PIECE)]
        copy = remote(source, cells.at[:, own_rows], send_d.at[i], recv_d.at[c], peer(o, s))
        copy.start()
        sent.append(copy)
    own_cells = pltpu.make_async_copy(columns.at[pl.ds(c * PIECE, PIECE)], cells.at[:, own_rows], own_sem.at[0])
    own_cells.start()

    for q in chips:
        source = sensed.at[pl.ds(0, NCOL)]
        remote(source, right.at[q, core], send_a.at[0], recv_a.at[q], peer(same_core(q), s)).wait_recv()
    swap = remote(right.at[:, core], right.at[:, core], send_a.at[3], recv_a.at[4], peer(partner, s))
    swap.start()
    swap.wait()
    part = lax.dot_general(
        sensed[...],
        right[...].reshape(KALL, OBS),
        (((1,), (1,)), ((), ())),
        precision=HIGH,
        preferred_element_type=jnp.float32,
    )
    block[...] = part
    for i, p in enumerate(planes):
        copy = remote(block, across.at[plane], send_b.at[i], recv_b.at[plane], peer(c, space_of(p)))
        copy.start()
        sent.append(copy)
    across[plane] = part
    for p in planes:
        remote(block, across.at[p], send_b.at[0], recv_b.at[p], peer(c, space_of(p))).wait_recv()
    total = across[0]
    for p in range(1, 16):
        total = total + across[p]
    layers[core, zh, chip] = total
    for i, (q, t, _) in enumerate(line):
        ours = layers.at[core, zh, chip]
        copy = remote(ours, ours, send_c.at[i], recv_c.at[zh, chip], peer(same_core(q), t))
        copy.start()
        sent.append(copy)
    for q, t, side in line:
        theirs = layers.at[core, side, q]
        remote(theirs, theirs, send_c.at[0], recv_c.at[side, q], peer(same_core(q), t)).wait_recv()
    swap = remote(layers.at[core], layers.at[core], send_c.at[7], recv_c.at[2, 0], peer(partner, s))
    swap.start()
    swap.wait()
    for o in range(NC):
        both = [layers[o % 2, side, o // 2, pl.ds(0, NCOL)] for side in range(2)]
        gram[pl.ds(o * NCOL, NCOL)] = both[0] + both[1]
    target = layers[0, 0, 0, pl.ds(NCOL, 8)][:1] + layers[0, 1, 0, pl.ds(NCOL, 8)][:1]
    factor(gram, stack)
    inverse = stack[:, KALL:]
    halfway = jnp.sum(inverse * target, axis=1, keepdims=True)
    weights = jnp.sum(halfway * inverse, axis=0, keepdims=True)
    w_hi = weights.astype(jnp.bfloat16).astype(jnp.float32)
    w_mid = (weights - w_hi).astype(jnp.bfloat16).astype(jnp.float32)
    w_low = weights - w_hi - w_mid
    row16 = lax.broadcasted_iota(jnp.int32, (NCOL, KALL), 0)
    extra = jnp.where(row16 == 0, w_hi, jnp.where(row16 == 1, w_mid, jnp.where(row16 == 2, w_low, 0.0)))
    transform = jnp.concatenate([inverse.astype(jnp.bfloat16), extra.astype(jnp.bfloat16)], axis=0)

    for o in others:
        source = columns.at[pl.ds(0, PIECE)]
        remote(source, cells.at[:, rows_of(o)], send_d.at[0], recv_d.at[o], peer(o, s)).wait_recv()
    own_cells.wait()
    for g in range(GROUPS):
        for fr in range(g * GROUP, (g + 1) * GROUP):
            out = jnp.dot(transform, cells[fr], preferred_element_type=jnp.float32)
            made[fr] = out[:KALL].astype(jnp.bfloat16)
            added[pl.ds(fr, 1)] = out[KALL : KALL + 1] + out[KALL + 1 : KALL + 2] + out[KALL + 2 : KALL + 3]
        some = pl.ds(g * GROUP, GROUP)
        goal = pl.ds(c * PIECE + g * GROUP, GROUP)
        for i, o in enumerate(others):
            copy = remote(
                made.at[some, rows_of(o)], result_ref.at[goal], send_e.at[g, i], recv_e.at[g, c], peer(o, s)
            )
            copy.start()
            sent.append(copy)
    for i, o in enumerate(others):
        copy = remote(added, increment_ref.at[c], send_f.at[i], recv_f.at[c], peer(o, s))
        copy.start()
        sent.append(copy)
    own_made = pltpu.make_async_copy(
        made.at[:, own_rows], result_ref.at[pl.ds(c * PIECE, PIECE)], own_sem.at[0]
    )
    own_made.start()
    increment_ref[c] = added[...]
    for o in others:
        for g in range(GROUPS):
            theirs = result_ref.at[pl.ds(o * PIECE + g * GROUP, GROUP)]
            some = pl.ds(g * GROUP, GROUP)
            remote(made.at[some, own_rows], theirs, send_e.at[0, 0], recv_e.at[g, o], peer(o, s)).wait_recv()
        remote(added, increment_ref.at[o], send_f.at[0], recv_f.at[o], peer(o, s)).wait_recv()
    own_made.wait()
    for copy in sent + shared:
        copy.wait_send()


def filter_step(cov, piece, land, stations, observed, weight):
    dma = pltpu.SemaphoreType.DMA
    f32, bf16 = jnp.float32, jnp.bfloat16
    return pl.pallas_call(
        filter_kernel,
        out_shape=(
            jax.ShapeDtypeStruct((FR, NCOL, WIDTH), bf16),
            jax.ShapeDtypeStruct((NC, NCOL, WIDTH), f32),
            jax.ShapeDtypeStruct((FR, WIDTH), f32),
        ),
        in_specs=[HBM, VMEM, HBM, HBM, HBM, HBM],
        out_specs=(VMEM, VMEM, VMEM),
        scratch_shapes=[
            pltpu.VMEM((NCOL, FR, WIDTH), f32),
            pltpu.VMEM((WIN, WIDTH), jnp.int32),
            pltpu.VMEM((1, OBS), jnp.int32),
            pltpu.VMEM((1, OBS), f32),
            pltpu.VMEM((1, OBS), f32),
            pltpu.VMEM((CHUNKS, EDGE, WIDTH), bf16),
            pltpu.VMEM((CHUNKS, EDGE, WIDTH), bf16),
            pltpu.VMEM((CHUNKS, EDGE, WIDTH), bf16),
            pltpu.VMEM((CHUNKS, EDGE, WIDTH), bf16),
            pltpu.VMEM((2, 4, 4, 12, 128), f32),
            pltpu.VMEM((4, 6 * HALO, WIDTH), f32),
            pltpu.VMEM((6 * STEPS, WIN, WIDTH), f32),
            pltpu.VMEM((2, NCOL * FR, 128), f32),
            pltpu.VMEM(((NCOL + 1) * TILE, WIDTH), f32),
            pltpu.VMEM((FR, NCOL, WIDTH), bf16),
            pltpu.VMEM((PIECE, KALL, WIDTH), bf16),
            pltpu.VMEM((NCOL + 8, OBS), f32),
            pltpu.VMEM((4, 2, NCOL, OBS), f32),
            pltpu.VMEM((NCOL + 8, KALL), f32),
            pltpu.VMEM((16, NCOL + 8, KALL), f32),
            pltpu.VMEM((2, 2, 4, NCOL + 8, KALL), f32),
            pltpu.VMEM((KALL, KALL), f32),
            pltpu.VMEM((KALL, 2 * KALL), f32),
            pltpu.VMEM((PIECE, KALL, WIDTH), bf16),
            pltpu.VMEM((NCOL, WIDTH), f32),
            dma((CHUNKS,)),
            dma((6,)),
            dma((2, CHUNKS)),
            dma((2, CHUNKS)),
            dma((2,)),
            dma((2,)),
            dma((4,)),
            dma((5,)),
            dma((4,)),
            dma((5,)),
            dma((15,)),
            dma((16,)),
            dma((8,)),
            dma((3, 4)),
            dma((NC - 1,)),
            dma((NC,)),
            dma((GROUPS, NC - 1)),
            dma((GROUPS, NC)),
            dma((NC - 1,)),
            dma((NC,)),
            dma((1,)),
        ],
        compiler_params=pltpu.CompilerParams(
            collective_id=0, has_side_effects=True, vmem_limit_bytes=60 * 1024 * 1024
        ),
        name="filter_step",
    )(cov, piece, land, stations, observed, weight)


PAIR = 2


def place_kernel(result_ref, increment_ref, meanf_ref, out_ref, mean_ref, held, total):
    j = pl.program_id(0)

    @pl.when(j == 0)
    def _():
        for half in range(2):
            part = result_ref[:, :, 128 * half : 128 * (half + 1)].astype(jnp.float32)
            held[half] = part.reshape(FR * NCOL, 128)
        for o in range(NC):
            rows = pl.ds(o * PIECE, PIECE)
            total[rows] = meanf_ref[rows] + increment_ref[o][:PIECE]
        c = lax.axis_index("cols")
        width = WIDTH // NC
        turned = pltpu.roll(total[...], lax.rem(WIDTH - c * width, WIDTH), 1)
        mean_ref[...] = turned[:, :width]

    for n in range(PAIR):
        for half in range(2):
            out_ref[n, :, 128 * half : 128 * (half + 1)] = held[half, pl.ds(j * PAIR + n, FR, stride=NCOL)]


def place(result, increment, mean_forecast):
    whole = lambda shape: pl.BlockSpec(shape, lambda i: (0,) * len(shape))
    return pl.pallas_call(
        place_kernel,
        grid=(NCOL // PAIR,),
        out_shape=(
            jax.ShapeDtypeStruct((NCOL, FR, WIDTH), jnp.float32),
            jax.ShapeDtypeStruct((FR, WIDTH // NC), jnp.float32),
        ),
        in_specs=[whole((FR, NCOL, WIDTH)), whole((NC, NCOL, WIDTH)), whole((FR, WIDTH))],
        out_specs=(pl.BlockSpec((PAIR, FR, WIDTH), lambda i: (i, 0, 0)), whole((FR, WIDTH // NC))),
        scratch_shapes=[pltpu.VMEM((2, FR * NCOL, 128), jnp.float32), pltpu.VMEM((FR, WIDTH), jnp.float32)],
        compiler_params=pltpu.CompilerParams(vmem_limit_bytes=24 * 1024 * 1024),
        name="place",
    )(result, increment, mean_forecast)


def local(mean_state, covariance, land_mask, stations, observed, obs_weight):
    width = WIDTH // NC
    halves = mean_state.reshape(6, 2, HALO, width).transpose(1, 0, 2, 3)
    piece = halves.reshape(2, 4, 12, width).transpose(0, 2, 1, 3).reshape(2, 12, 128)
    result, increment, mean_forecast = filter_step(
        covariance.reshape(NCOL, FR, WIDTH), piece, land_mask, stations[None], observed[None], obs_weight[None]
    )
    updated, mean = place(result, increment, mean_forecast)
    return mean.reshape(mean_state.shape), updated.reshape(covariance.shape)


def solution(mesh):
    return jax.shard_map(
        local,
        mesh=mesh,
        in_specs=(
            P(None, "space", "cols"),
            P("cols", None, "space", None),
            P(),
            P("space"),
            P("space"),
            P("space"),
        ),
        out_specs=(P(None, "space", "cols"), P("cols", None, "space", None)),
        check_vma=False,
    )
```

```python
import jax
import jax.numpy as jnp
from jax import lax
from jax.experimental import pallas as pl
from jax.experimental.pallas import tpu as pltpu
from jax.sharding import PartitionSpec as P

STEPS = 4
HALO = 8
TILE = 16
WIN = TILE + 2 * HALO
NC = 8
NS = 32
NCOL = 16
KALL = 128
WIDTH = 256
FR = 96
PIECE = 12
OBS = 128

HIGH = lax.Precision.HIGHEST
MESH = pl.DeviceIdType.MESH
ANY = pl.BlockSpec(memory_space=pl.ANY)
VMEM = pl.BlockSpec(memory_space=pltpu.VMEM)
HBM = pl.BlockSpec(memory_space=pltpu.HBM)


def peer(c, s):
    return {"cols": c, "space": s}


def greet(peers):
    barrier = pltpu.get_barrier_semaphore()
    for device in peers:
        pl.semaphore_signal(barrier, inc=1, device_id=device, device_id_type=MESH)
    pl.semaphore_wait(barrier, len(peers))


def remote(src, dst, send, recv, device):
    return pltpu.make_async_remote_copy(
        src_ref=src, dst_ref=dst, send_sem=send, recv_sem=recv, device_id=device, device_id_type=MESH
    )


def row_difference(a):
    rows = a.shape[0]
    return pltpu.roll(a, rows - 1, 0) - pltpu.roll(a, 1, 0)


def col_difference(a, first, last):
    width = a.shape[1]
    after = jnp.where(last, 0.0, pltpu.roll(a, width - 1, 1))
    before = jnp.where(first, 0.0, pltpu.roll(a, 1, 1))
    return after - before


def new_velocities(fields, wet, first, last):
    top_pressure = fields[0] + fields[3]
    pressures = (top_pressure, top_pressure - 0.125 * fields[0])
    pairs = []
    for layer in range(2):
        u, v = fields[3 * layer + 1], fields[3 * layer + 2]
        p = pressures[layer]
        u_new = wet * (0.975 * u + 0.15 * v - 0.25 * row_difference(p))
        v_new = wet * (0.975 * v - 0.15 * u - 0.25 * col_difference(p, first, last))
        pairs.append((u_new, v_new))
    return pairs


BLOCK = 32


def factor(gram, stack):
    stack[...] = jnp.zeros(stack.shape, jnp.float32)
    row = lax.broadcasted_iota(jnp.int32, (BLOCK, KALL), 0)
    lane = lax.broadcasted_iota(jnp.int32, (BLOCK, KALL), 1)

    def one(b, carry):
        start = pl.multiple_of(b * BLOCK, BLOCK)
        back = lax.rem(KALL - start, KALL)
        done = stack[...]
        turned = pltpu.roll(done[:, :KALL], back, 1)
        product = lax.dot_general(
            turned, done, (((0,), (0,)), ((), ())), precision=HIGH, preferred_element_type=jnp.float32
        )[:BLOCK]
        eye = (lane == row + start).astype(jnp.float32)
        left = gram[pl.ds(start, BLOCK)] + eye - product[:, :KALL]
        right = eye - product[:, KALL:]
        square = pltpu.roll(left, back, 1)
        cols = [jnp.broadcast_to(square[:, m : m + 1], (BLOCK, KALL)) for m in range(BLOCK)]
        scale = jnp.zeros((BLOCK, KALL), jnp.float32)
        for j in range(BLOCK):
            r = lax.rsqrt(cols[j][j : j + 1])
            col = cols[j] * r
            strict = jnp.where(row > j, col, 0.0)
            for m in range(j + 1, BLOCK):
                cols[m] = cols[m] - strict * col[m : m + 1]
            left = left - strict * (left[j : j + 1] * r)
            right = right - strict * (right[j : j + 1] * r)
            scale = jnp.where(row == j, r, scale)
        stack[pl.ds(start, BLOCK), :KALL] = left * scale
        stack[pl.ds(start, BLOCK), KALL:] = right * scale
        return carry

    lax.fori_loop(0, KALL // BLOCK, one, 0)


CHUNKS = 8
FIRST = 4
ON0, FAR1, ON1 = 0, 1, 4
PER = NCOL // CHUNKS
EDGE = PER * 6 * HALO
GROUPS = 4
GROUP = PIECE // GROUPS


def filter_kernel(
    cov_ref, mean_hbm, land_ref, stations_hbm, observed_hbm, weight_hbm,
    result_ref, increment_ref, meanf_ref,
    cov, wet_rows, stations_ref, observed_ref, weight_ref, low, high, above, below, relay, mean_in, mean_rows, piece_ref, pieces, wide, carried, held, surface, columns, cells,
    sensed, right, block, across, layers, gram, stack, made, added,
    load_sem, small_sem, halo_send, halo_recv, relay_send, relay_recv, m_send, m_recv,
    send_a, recv_a, send_b, recv_b, send_c, recv_c, send_d, recv_d, send_e, recv_e, send_f, recv_f, own_sem,
):
    c = lax.axis_index("cols")
    s = lax.axis_index("space")
    down, up = lax.rem(s + 1, NS), lax.rem(s + NS - 1, NS)
    y, zh, x = s // 8, lax.rem(s // 4, 2), lax.rem(s, 4)
    plane = y * 4 + x
    others = [lax.rem(c + i, NC) for i in range(1, NC)]
    planes = [lax.rem(plane + i, 16) for i in range(1, 16)]
    space_of = lambda p: (p // 4) * 8 + zh * 4 + lax.rem(p, 4)
    far = y * 8 + (1 - zh) * 4 + x
    chip, core = c // 2, lax.rem(c, 2)
    partner = 2 * chip + 1 - core
    chips = [lax.rem(chip + i, 4) for i in range(1, 4)]
    line = [(q, s, zh) for q in chips] + [(q, far, 1 - zh) for q in [chip] + chips]
    same_core = lambda q: 2 * q + core

    peers = [peer(same_core(q), t) for t in (down, up) for q in [chip] + chips] + [peer(o, s) for o in others]
    peers += [peer(same_core(q), far) for q in [chip] + chips] + [peer(c, space_of(p)) for p in planes]
    barrier = pltpu.get_barrier_semaphore()
    for device in peers:
        pl.semaphore_signal(barrier, inc=1, device_id=device, device_id_type=MESH)

    def load(i):
        at = pl.ds(pl.multiple_of(i * PER, PER), PER)
        return pltpu.make_async_copy(cov_ref.at[at], cov.at[at], load_sem.at[i])

    def start_load(i, carry):
        load(i).start()
        return carry

    top_row = pl.multiple_of(jnp.maximum(s * TILE - HALO, 0), HALO)
    end_row = pl.multiple_of(jnp.minimum(s * TILE + TILE, NS * TILE - HALO), HALO)
    own_row = pl.multiple_of(s * TILE, TILE)
    smalls = [
        pltpu.make_async_copy(land_ref.at[pl.ds(top_row, HALO)], wet_rows.at[pl.ds(0, HALO)], small_sem.at[0]),
        pltpu.make_async_copy(land_ref.at[pl.ds(own_row, TILE)], wet_rows.at[pl.ds(HALO, TILE)], small_sem.at[1]),
        pltpu.make_async_copy(
            land_ref.at[pl.ds(end_row, HALO)], wet_rows.at[pl.ds(HALO + TILE, HALO)], small_sem.at[2]
        ),
        pltpu.make_async_copy(stations_hbm, stations_ref, small_sem.at[3]),
        pltpu.make_async_copy(observed_hbm, observed_ref, small_sem.at[4]),
        pltpu.make_async_copy(weight_hbm, weight_ref, small_sem.at[5]),
    ]
    load_mean = pltpu.make_async_copy(mean_hbm, mean_in, small_sem.at[6])
    load_mean.start()
    lax.fori_loop(0, CHUNKS, start_load, 0)
    for copy in smalls:
        copy.start()
    load_mean.wait()
    for part in range(2):
        for f in range(6):
            mean_rows[part, pl.ds(HALO * f, HALO)] = mean_in[f, pl.ds(HALO * part, HALO)]
        packed = jnp.concatenate([mean_rows[part, pl.ds(12 * q, 12)] for q in range(4)], axis=1)
        piece_ref[part] = packed
        pieces[core, chip, 1 + part] = packed

    def convert(i):
        for n in range(PER):
            k = i * PER + n
            rows = pl.ds(n * 6 * HALO, 6 * HALO)
            upper = [cov[k, pl.ds(TILE * f, HALO)] for f in range(6)]
            lower = [cov[k, pl.ds(TILE * f + HALO, HALO)] for f in range(6)]
            low[i, rows] = jnp.concatenate(upper, axis=0).astype(jnp.bfloat16)
            high[i, rows] = jnp.concatenate(lower, axis=0).astype(jnp.bfloat16)

    def to_down(i):
        return remote(high.at[i], above.at[i], halo_send.at[0, i], halo_recv.at[0, i], peer(c, down))

    run = y * 8 + zh * 4
    between = (x == 1) | (x == 2)
    next_run = jnp.where(zh == 1, y * 8 + 4, lax.rem(y + 1, 4) * 8)
    last_run = jnp.where(zh == 0, y * 8 + 3, lax.rem(y + 3, 4) * 8 + 7)

    def start_halo(i):
        odd = lax.rem(i, 2) == 1
        slot = i // 4
        inner = peer(c, run + 1 + lax.rem(i // 2, 2))

        def one(way, end, direct, source):
            @pl.when(odd & end)
            def _():
                at = relay.at[0, way, slot]
                remote(source.at[i], at, halo_send.at[way, i], relay_recv.at[0, way, slot], inner).start()

            @pl.when(jnp.logical_not(odd & end))
            def _():
                direct(i).start()

        one(0, x == 3, to_down, high)
        one(1, x == 0, to_up, low)

    def relay_far(way, slot):
        return remote(
            relay.at[0, way, slot], relay.at[1, way, slot],
            relay_send.at[0, way, slot], relay_recv.at[1, way, slot], peer(c, far),
        )

    def relay_on(way, slot):
        i = 4 * slot + 2 * x - 1
        goal = (above, below)[way].at[i]
        device = peer(c, (next_run, last_run)[way])
        return remote(relay.at[1, way, slot], goal, relay_send.at[1, way, slot], halo_recv.at[way, i], device)

    def pass_far(slot):
        @pl.when(between)
        def _():
            for way in range(2):
                source = (high, low)[way].at[0]
                recv = relay_recv.at[0, way, slot]
                remote(source, relay.at[0, way, slot], halo_send.at[way, 0], recv, peer(c, down)).wait_recv()
                relay_far(way, slot).start()

    def pass_on(slot):
        @pl.when(between)
        def _():
            for way in range(2):
                relay_far(way, slot).wait_recv()
                relay_on(way, slot).start()

    def to_up(i):
        return remote(low.at[i], below.at[i], halo_send.at[1, i], halo_recv.at[1, i], peer(c, up))

    load(0).wait()
    convert(0)
    pl.semaphore_wait(barrier, len(peers))
    shared = []
    for i, q in enumerate([chip] + chips):
        device = same_core(q)
        to = lambda kind: (m_send.at[kind, i], m_recv.at[kind, chip])
        shared.append(remote(piece_ref.at[1], pieces.at[core, chip, 0], *to(0), peer(device, down)))
        shared.append(remote(piece_ref.at[0], pieces.at[core, chip, 3], *to(2), peer(device, up)))
        if i:
            shared.append(remote(piece_ref, pieces.at[core, chip, pl.ds(1, 2)], *to(1), peer(device, s)))
    for copy in shared:
        copy.start()
    start_halo(0)

    def send_halo(i, carry):
        load(i).wait()
        convert(i)

        @pl.when(i < FIRST)
        def _():
            start_halo(i)

        return carry

    lax.fori_loop(1, CHUNKS, send_halo, 0)
    pass_far(0)

    def send_more(i, carry):
        to_down(i - FIRST).wait_send()
        to_up(i - FIRST).wait_send()
        start_halo(i)
        return carry

    lax.fori_loop(FIRST, CHUNKS, send_more, 0)

    lane = lax.broadcasted_iota(jnp.int32, (WIN, WIDTH), 1)
    first, last = lane == 0, lane == WIDTH - 1
    grid_row = s * TILE - HALO + lax.broadcasted_iota(jnp.int32, (WIN, WIDTH), 0)
    inside = ((grid_row >= 0) & (grid_row < NS * TILE)).astype(jnp.float32)
    for copy in smalls:
        copy.wait()
    wet = wet_rows[...].astype(jnp.float32) * inside
    for i, q in enumerate([chip] + chips):
        device = peer(same_core(q), down)
        remote(piece_ref.at[1], pieces.at[core, q, 0], m_send.at[0, 0], m_recv.at[0, q], device).wait_recv()
        remote(piece_ref.at[0], pieces.at[core, q, 3], m_send.at[0, 0], m_recv.at[2, q], device).wait_recv()
        if i:
            theirs = pieces.at[core, q, pl.ds(1, 2)]
            remote(piece_ref, theirs, m_send.at[0, 0], m_recv.at[1, q], device).wait_recv()
    swap = remote(pieces.at[core], pieces.at[core], m_send.at[1, 0], m_recv.at[1, chip], peer(partner, s))
    swap.start()
    swap.wait()
    quarter = lax.broadcasted_iota(jnp.int32, (12, 128), 1) // 32
    for slot in range(4):
        for half in range(2):
            for q in range(4):
                rows = jnp.zeros((12, 128), jnp.float32)
                for p in range(4):
                    value = pieces[p % 2, 2 * half + p // 2, slot]
                    value = pltpu.roll(value, (32 * (p - q)) % 128, 1) if p != q else value
                    rows = jnp.where(quarter == p, value, rows)
                wide[slot, pl.ds(12 * q, 12), 128 * half : 128 * (half + 1)] = rows
    fields = []
    for f in range(6):
        rows = [wide[slot, pl.ds(HALO * f, HALO)] for slot in range(4)]
        fields.append(jnp.concatenate(rows, axis=0) * inside)
    for step in range(STEPS):
        pairs = new_velocities(fields, wet, first, last)
        after = []
        for layer in range(2):
            h = fields[3 * layer]
            depth = (1.0, 2.0)[layer] + h
            u, v = pairs[layer]
            base = 6 * step + 3 * layer
            carried[base] = depth
            carried[base + 1] = u
            carried[base + 2] = v
            h_new = inside * (h - 0.25 * (row_difference(depth * u) + col_difference(depth * v, first, last)))
            after += [h_new, u, v]
        fields = after
    for f in range(6):
        meanf_ref[pl.ds(TILE * f, TILE)] = fields[f][HALO : HALO + TILE]
    surface[pl.ds(NCOL * TILE, TILE)] = (fields[0] + fields[3])[HALO : HALO + TILE]

    def advance(i, carry):
        for at, action, slot in ((ON0, pass_on, 0), (FAR1, pass_far, 1), (ON1, pass_on, 1)):

            @pl.when(i == at)
            def _():
                action(slot)

        to_down(i).wait_recv()
        to_up(i).wait_recv()
        for n in range(PER):
            k = i * PER + n
            rows = pl.ds(n * 6 * HALO, 6 * HALO)
            before = above[i, rows].astype(jnp.float32)
            behind = below[i, rows].astype(jnp.float32)
            fields = []
            for f in range(6):
                parts = [
                    before[HALO * f : HALO * (f + 1)],
                    cov[k, pl.ds(TILE * f, TILE)],
                    behind[HALO * f : HALO * (f + 1)],
                ]
                fields.append(jnp.concatenate(parts, axis=0) * inside)
            for step in range(STEPS):
                pairs = new_velocities(fields, wet, first, last)
                after = []
                for layer in range(2):
                    h = fields[3 * layer]
                    u, v = pairs[layer]
                    base = 6 * step + 3 * layer
                    depth = carried[base]
                    rows_flux = depth * u + h * carried[base + 1]
                    cols_flux = depth * v + h * carried[base + 2]
                    change = row_difference(rows_flux) + col_difference(cols_flux, first, last)
                    after += [inside * (h - 0.25 * change), u, v]
                fields = after
            for f in range(6):
                at = pl.ds(pl.multiple_of(k * FR + TILE * f, TILE), TILE)
                for half in range(2):
                    held[half, at] = fields[f][HALO : HALO + TILE, 128 * half : 128 * (half + 1)]
            surface[pl.ds(pl.multiple_of(k * TILE, TILE), TILE)] = (fields[0] + fields[3])[HALO : HALO + TILE]
        return carry

    lax.fori_loop(0, CHUNKS, advance, 0)

    cell = stations_ref[...] - s * (TILE * WIDTH)
    pick = (lax.broadcasted_iota(jnp.int32, (WIDTH, OBS), 0) == cell % WIDTH).astype(jnp.float32)
    at_rows = lax.broadcasted_iota(jnp.int32, (TILE, OBS), 0) == cell // WIDTH
    picked = jnp.dot(surface[...], pick, precision=HIGH, preferred_element_type=jnp.float32)
    picked = picked.reshape(NCOL + 1, TILE, OBS)
    values = jnp.sum(jnp.where(at_rows[None], picked, 0.0), axis=1)
    weight = weight_ref[...]
    mine = values[:NCOL] * weight
    innovation = weight * (observed_ref[...] - values[NCOL:])
    below_first = lax.broadcasted_iota(jnp.int32, (8, OBS), 0) > 0
    sensed[pl.ds(0, NCOL)] = mine
    sensed[pl.ds(NCOL, 8)] = jnp.where(below_first, 0.0, jnp.broadcast_to(innovation, (8, OBS)))
    own_rows = pl.ds(pl.multiple_of(c * NCOL, NCOL), NCOL)
    rows_of = lambda o: pl.ds(pl.multiple_of(o * NCOL, NCOL), NCOL)
    sent = []
    for i, q in enumerate(chips):
        source = sensed.at[pl.ds(0, NCOL)]
        copy = remote(source, right.at[chip, core], send_a.at[i], recv_a.at[chip], peer(same_core(q), s))
        copy.start()
        sent.append(copy)
    right[chip, core] = mine

    def gather_row(fr, carry):
        for half in range(2):
            value = held[half, pl.ds(fr, NCOL, stride=FR)]
            columns[fr, :, 128 * half : 128 * (half + 1)] = value.astype(jnp.bfloat16)
        return carry

    lax.fori_loop(0, FR, gather_row, 0, unroll=8)
    for i, o in enumerate(others):
        source = columns.at[pl.ds(o * PIECE, PIECE)]
        copy = remote(source, cells.at[:, own_rows], send_d.at[i], recv_d.at[c], peer(o, s))
        copy.start()
        sent.append(copy)
    own_cells = pltpu.make_async_copy(columns.at[pl.ds(c * PIECE, PIECE)], cells.at[:, own_rows], own_sem.at[0])
    own_cells.start()

    for q in chips:
        source = sensed.at[pl.ds(0, NCOL)]
        remote(source, right.at[q, core], send_a.at[0], recv_a.at[q], peer(same_core(q), s)).wait_recv()
    swap = remote(right.at[:, core], right.at[:, core], send_a.at[3], recv_a.at[4], peer(partner, s))
    swap.start()
    swap.wait()
    part = lax.dot_general(
        sensed[...],
        right[...].reshape(KALL, OBS),
        (((1,), (1,)), ((), ())),
        precision=HIGH,
        preferred_element_type=jnp.float32,
    )
    block[...] = part
    for i, p in enumerate(planes):
        copy = remote(block, across.at[plane], send_b.at[i], recv_b.at[plane], peer(c, space_of(p)))
        copy.start()
        sent.append(copy)
    across[plane] = part
    for p in planes:
        remote(block, across.at[p], send_b.at[0], recv_b.at[p], peer(c, space_of(p))).wait_recv()
    total = across[0]
    for p in range(1, 16):
        total = total + across[p]
    layers[core, zh, chip] = total
    for i, (q, t, _) in enumerate(line):
        ours = layers.at[core, zh, chip]
        copy = remote(ours, ours, send_c.at[i], recv_c.at[zh, chip], peer(same_core(q), t))
        copy.start()
        sent.append(copy)
    for q, t, side in line:
        theirs = layers.at[core, side, q]
        remote(theirs, theirs, send_c.at[0], recv_c.at[side, q], peer(same_core(q), t)).wait_recv()
    swap = remote(layers.at[core], layers.at[core], send_c.at[7], recv_c.at[2, 0], peer(partner, s))
    swap.start()
    swap.wait()
    for o in range(NC):
        both = [layers[o % 2, side, o // 2, pl.ds(0, NCOL)] for side in range(2)]
        gram[pl.ds(o * NCOL, NCOL)] = both[0] + both[1]
    target = layers[0, 0, 0, pl.ds(NCOL, 8)][:1] + layers[0, 1, 0, pl.ds(NCOL, 8)][:1]
    factor(gram, stack)
    inverse = stack[:, KALL:]
    halfway = jnp.sum(inverse * target, axis=1, keepdims=True)
    weights = jnp.sum(halfway * inverse, axis=0, keepdims=True)
    w_hi = weights.astype(jnp.bfloat16).astype(jnp.float32)
    w_mid = (weights - w_hi).astype(jnp.bfloat16).astype(jnp.float32)
    w_low = weights - w_hi - w_mid
    row16 = lax.broadcasted_iota(jnp.int32, (NCOL, KALL), 0)
    extra = jnp.where(row16 == 0, w_hi, jnp.where(row16 == 1, w_mid, jnp.where(row16 == 2, w_low, 0.0)))
    transform = jnp.concatenate([inverse.astype(jnp.bfloat16), extra.astype(jnp.bfloat16)], axis=0)

    for o in others:
        source = columns.at[pl.ds(0, PIECE)]
        remote(source, cells.at[:, rows_of(o)], send_d.at[0], recv_d.at[o], peer(o, s)).wait_recv()
    own_cells.wait()
    for g in range(GROUPS):
        for fr in range(g * GROUP, (g + 1) * GROUP):
            out = jnp.dot(transform, cells[fr], preferred_element_type=jnp.float32)
            made[fr] = out[:KALL].astype(jnp.bfloat16)
            added[pl.ds(fr, 1)] = out[KALL : KALL + 1] + out[KALL + 1 : KALL + 2] + out[KALL + 2 : KALL + 3]
        some = pl.ds(g * GROUP, GROUP)
        goal = pl.ds(c * PIECE + g * GROUP, GROUP)
        for i, o in enumerate(others):
            copy = remote(
                made.at[some, rows_of(o)], result_ref.at[goal], send_e.at[g, i], recv_e.at[g, c], peer(o, s)
            )
            copy.start()
            sent.append(copy)
    for i, o in enumerate(others):
        copy = remote(added, increment_ref.at[c], send_f.at[i], recv_f.at[c], peer(o, s))
        copy.start()
        sent.append(copy)
    own_made = pltpu.make_async_copy(
        made.at[:, own_rows], result_ref.at[pl.ds(c * PIECE, PIECE)], own_sem.at[0]
    )
    own_made.start()
    increment_ref[c] = added[...]
    for o in others:
        for g in range(GROUPS):
            theirs = result_ref.at[pl.ds(o * PIECE + g * GROUP, GROUP)]
            some = pl.ds(g * GROUP, GROUP)
            remote(made.at[some, own_rows], theirs, send_e.at[0, 0], recv_e.at[g, o], peer(o, s)).wait_recv()
        remote(added, increment_ref.at[o], send_f.at[0], recv_f.at[o], peer(o, s)).wait_recv()
    own_made.wait()
    for copy in sent + shared:
        copy.wait_send()

    def wait_halo(i, carry):
        to_down(i).wait_send()
        to_up(i).wait_send()
        return carry

    lax.fori_loop(CHUNKS - FIRST, CHUNKS, wait_halo, 0)

    @pl.when(between)
    def _():
        for way in range(2):
            for slot in range(2):
                relay_far(way, slot).wait_send()
                relay_on(way, slot).wait_send()


def filter_step(cov, mean, land, stations, observed, weight):
    dma = pltpu.SemaphoreType.DMA
    f32, bf16 = jnp.float32, jnp.bfloat16
    return pl.pallas_call(
        filter_kernel,
        out_shape=(
            jax.ShapeDtypeStruct((FR, NCOL, WIDTH), bf16),
            jax.ShapeDtypeStruct((NC, NCOL, WIDTH), f32),
            jax.ShapeDtypeStruct((FR, WIDTH), f32),
        ),
        in_specs=[HBM] * 6,
        out_specs=(VMEM, VMEM, VMEM),
        scratch_shapes=[
            pltpu.VMEM((NCOL, FR, WIDTH), f32),
            pltpu.VMEM((WIN, WIDTH), jnp.int32),
            pltpu.VMEM((1, OBS), jnp.int32),
            pltpu.VMEM((1, OBS), f32),
            pltpu.VMEM((1, OBS), f32),
            pltpu.VMEM((CHUNKS, EDGE, WIDTH), bf16),
            pltpu.VMEM((CHUNKS, EDGE, WIDTH), bf16),
            pltpu.VMEM((CHUNKS, EDGE, WIDTH), bf16),
            pltpu.VMEM((CHUNKS, EDGE, WIDTH), bf16),
            pltpu.VMEM((2, 2, 2, EDGE, WIDTH), bf16),
            pltpu.VMEM((6, TILE, WIDTH // NC), f32),
            pltpu.VMEM((2, 6 * HALO, WIDTH // NC), f32),
            pltpu.VMEM((2, 12, 128), f32),
            pltpu.VMEM((2, 4, 4, 12, 128), f32),
            pltpu.VMEM((4, 6 * HALO, WIDTH), f32),
            pltpu.VMEM((6 * STEPS, WIN, WIDTH), f32),
            pltpu.VMEM((2, NCOL * FR, 128), f32),
            pltpu.VMEM(((NCOL + 1) * TILE, WIDTH), f32),
            pltpu.VMEM((FR, NCOL, WIDTH), bf16),
            pltpu.VMEM((PIECE, KALL, WIDTH), bf16),
            pltpu.VMEM((NCOL + 8, OBS), f32),
            pltpu.VMEM((4, 2, NCOL, OBS), f32),
            pltpu.VMEM((NCOL + 8, KALL), f32),
            pltpu.VMEM((16, NCOL + 8, KALL), f32),
            pltpu.VMEM((2, 2, 4, NCOL + 8, KALL), f32),
            pltpu.VMEM((KALL, KALL), f32),
            pltpu.VMEM((KALL, 2 * KALL), f32),
            pltpu.VMEM((PIECE, KALL, WIDTH), bf16),
            pltpu.VMEM((NCOL, WIDTH), f32),
            dma((CHUNKS,)),
            dma((7,)),
            dma((2, CHUNKS)),
            dma((2, CHUNKS)),
            dma((2, 2, 2)),
            dma((2, 2, 2)),
            dma((3, 4)),
            dma((3, 4)),
            dma((4,)),
            dma((5,)),
            dma((15,)),
            dma((16,)),
            dma((8,)),
            dma((3, 4)),
            dma((NC - 1,)),
            dma((NC,)),
            dma((GROUPS, NC - 1)),
            dma((GROUPS, NC)),
            dma((NC - 1,)),
            dma((NC,)),
            dma((1,)),
        ],
        compiler_params=pltpu.CompilerParams(
            collective_id=0, has_side_effects=True, vmem_limit_bytes=60 * 1024 * 1024
        ),
        name="filter_step",
    )(cov, mean, land, stations, observed, weight)


PAIR = 2


def place_kernel(result_ref, increment_ref, meanf_ref, out_ref, mean_ref, held, total):
    j = pl.program_id(0)

    @pl.when(j == 0)
    def _():
        for half in range(2):
            part = result_ref[:, :, 128 * half : 128 * (half + 1)].astype(jnp.float32)
            held[half] = part.reshape(FR * NCOL, 128)
        for o in range(NC):
            rows = pl.ds(o * PIECE, PIECE)
            total[rows] = meanf_ref[rows] + increment_ref[o][:PIECE]
        c = lax.axis_index("cols")
        width = WIDTH // NC
        turned = pltpu.roll(total[...], lax.rem(WIDTH - c * width, WIDTH), 1)
        mean_ref[...] = turned[:, :width]

    for n in range(PAIR):
        for half in range(2):
            out_ref[n, :, 128 * half : 128 * (half + 1)] = held[half, pl.ds(j * PAIR + n, FR, stride=NCOL)]


def place(result, increment, mean_forecast):
    whole = lambda shape: pl.BlockSpec(shape, lambda i: (0,) * len(shape))
    return pl.pallas_call(
        place_kernel,
        grid=(NCOL // PAIR,),
        out_shape=(
            jax.ShapeDtypeStruct((NCOL, FR, WIDTH), jnp.float32),
            jax.ShapeDtypeStruct((FR, WIDTH // NC), jnp.float32),
        ),
        in_specs=[whole((FR, NCOL, WIDTH)), whole((NC, NCOL, WIDTH)), whole((FR, WIDTH))],
        out_specs=(pl.BlockSpec((PAIR, FR, WIDTH), lambda i: (i, 0, 0)), whole((FR, WIDTH // NC))),
        scratch_shapes=[pltpu.VMEM((2, FR * NCOL, 128), jnp.float32), pltpu.VMEM((FR, WIDTH), jnp.float32)],
        compiler_params=pltpu.CompilerParams(vmem_limit_bytes=60 * 1024 * 1024),
        name="place",
    )(result, increment, mean_forecast)


def local(mean_state, covariance, land_mask, stations, observed, obs_weight):
    result, increment, mean_forecast = filter_step(
        covariance.reshape(NCOL, FR, WIDTH), mean_state, land_mask, stations[None], observed[None], obs_weight[None]
    )
    updated, mean = place(result, increment, mean_forecast)
    return mean.reshape(mean_state.shape), updated.reshape(covariance.shape)


def solution(mesh):
    return jax.shard_map(
        local,
        mesh=mesh,
        in_specs=(
            P(None, "space", "cols"),
            P("cols", None, "space", None),
            P(),
            P("space"),
            P("space"),
            P("space"),
        ),
        out_specs=(P(None, "space", "cols"), P("cols", None, "space", None)),
        check_vma=False,
    )
```

```python
import jax
import jax.numpy as jnp
from jax import lax
from jax.experimental import pallas as pl
from jax.experimental.pallas import tpu as pltpu
from jax.sharding import PartitionSpec as P

STEPS = 4
HALO = 8
TILE = 16
WIN = TILE + 2 * HALO
NC = 8
NS = 32
NCOL = 16
KALL = 128
WIDTH = 256
FR = 96
PIECE = 12
OBS = 128

HIGH = lax.Precision.HIGHEST
MESH = pl.DeviceIdType.MESH
ANY = pl.BlockSpec(memory_space=pl.ANY)
VMEM = pl.BlockSpec(memory_space=pltpu.VMEM)
HBM = pl.BlockSpec(memory_space=pltpu.HBM)


def peer(c, s):
    return {"cols": c, "space": s}


def remote(src, dst, send, recv, device):
    return pltpu.make_async_remote_copy(
        src_ref=src, dst_ref=dst, send_sem=send, recv_sem=recv, device_id=device, device_id_type=MESH
    )


def row_difference(a):
    rows = a.shape[0]
    return pltpu.roll(a, rows - 1, 0) - pltpu.roll(a, 1, 0)


def col_difference(a, first, last):
    width = a.shape[1]
    after = jnp.where(last, 0.0, pltpu.roll(a, width - 1, 1))
    before = jnp.where(first, 0.0, pltpu.roll(a, 1, 1))
    return after - before


def new_velocities(fields, wet, first, last):
    top_pressure = fields[0] + fields[3]
    pressures = (top_pressure, top_pressure - 0.125 * fields[0])
    pairs = []
    for layer in range(2):
        u, v = fields[3 * layer + 1], fields[3 * layer + 2]
        p = pressures[layer]
        u_new = wet * (0.975 * u + 0.15 * v - 0.25 * row_difference(p))
        v_new = wet * (0.975 * v - 0.15 * u - 0.25 * col_difference(p, first, last))
        pairs.append((u_new, v_new))
    return pairs


BLOCK = 32


def factor(gram, stack):
    stack[...] = jnp.zeros(stack.shape, jnp.float32)
    row = lax.broadcasted_iota(jnp.int32, (BLOCK, KALL), 0)
    lane = lax.broadcasted_iota(jnp.int32, (BLOCK, KALL), 1)

    def one(b, carry):
        start = pl.multiple_of(b * BLOCK, BLOCK)
        back = lax.rem(KALL - start, KALL)
        done = stack[...]
        turned = pltpu.roll(done[:, :KALL], back, 1)
        product = lax.dot_general(
            turned, done, (((0,), (0,)), ((), ())), precision=HIGH, preferred_element_type=jnp.float32
        )[:BLOCK]
        eye = (lane == row + start).astype(jnp.float32)
        left = gram[pl.ds(start, BLOCK)] + eye - product[:, :KALL]
        right = eye - product[:, KALL:]
        square = pltpu.roll(left, back, 1)
        cols = [jnp.broadcast_to(square[:, m : m + 1], (BLOCK, KALL)) for m in range(BLOCK)]
        scale = jnp.zeros((BLOCK, KALL), jnp.float32)
        for j in range(BLOCK):
            r = lax.rsqrt(cols[j][j : j + 1])
            col = cols[j] * r
            strict = jnp.where(row > j, col, 0.0)
            for m in range(j + 1, BLOCK):
                cols[m] = cols[m] - strict * col[m : m + 1]
            left = left - strict * (left[j : j + 1] * r)
            right = right - strict * (right[j : j + 1] * r)
            scale = jnp.where(row == j, r, scale)
        stack[pl.ds(start, BLOCK), :KALL] = left * scale
        stack[pl.ds(start, BLOCK), KALL:] = right * scale
        return carry

    lax.fori_loop(0, KALL // BLOCK, one, 0)


CHUNKS = 8
FIRST = 8
ON0, ON1 = 0, 1
PER = NCOL // CHUNKS
EDGE = PER * 6 * HALO
GROUPS = 4
GROUP = PIECE // GROUPS


def filter_kernel(
    cov_ref, mean_hbm, land_ref, stations_hbm, observed_hbm, weight_hbm,
    result_ref, increment_ref, meanf_ref,
    cov, wet_rows, stations_ref, observed_ref, weight_ref, low, high, above, below, relay, mean_in, mean_rows, piece_ref, pieces, wide, carried, held, surface, columns, cells,
    sensed, right, block, across, layers, gram, stack, made, added,
    load_sem, small_sem, halo_send, halo_recv, relay_send, relay_recv, m_send, m_recv,
    send_a, recv_a, send_b, recv_b, send_c, recv_c, send_d, recv_d, send_e, recv_e, send_f, recv_f, own_sem,
):
    c = lax.axis_index("cols")
    s = lax.axis_index("space")
    down, up = lax.rem(s + 1, NS), lax.rem(s + NS - 1, NS)
    y, zh, x = s // 8, lax.rem(s // 4, 2), lax.rem(s, 4)
    plane = y * 4 + x
    others = [lax.rem(c + i, NC) for i in range(1, NC)]
    planes = [lax.rem(plane + i, 16) for i in range(1, 16)]
    space_of = lambda p: (p // 4) * 8 + zh * 4 + lax.rem(p, 4)
    far = y * 8 + (1 - zh) * 4 + x
    chip, core = c // 2, lax.rem(c, 2)
    partner = 2 * chip + 1 - core
    chips = [lax.rem(chip + i, 4) for i in range(1, 4)]
    line = [(q, s, zh) for q in chips] + [(q, far, 1 - zh) for q in [chip] + chips]
    same_core = lambda q: 2 * q + core

    peers = [peer(same_core(q), t) for t in (down, up) for q in [chip] + chips] + [peer(o, s) for o in others]
    peers += [peer(same_core(q), far) for q in [chip] + chips] + [peer(c, space_of(p)) for p in planes]
    barrier = pltpu.get_barrier_semaphore()
    for device in peers:
        pl.semaphore_signal(barrier, inc=1, device_id=device, device_id_type=MESH)

    def load(i):
        at = pl.ds(pl.multiple_of(i * PER, PER), PER)
        return pltpu.make_async_copy(cov_ref.at[at], cov.at[at], load_sem.at[i])

    def start_load(i, carry):
        load(i).start()
        return carry

    top_row = pl.multiple_of(jnp.maximum(s * TILE - HALO, 0), HALO)
    end_row = pl.multiple_of(jnp.minimum(s * TILE + TILE, NS * TILE - HALO), HALO)
    own_row = pl.multiple_of(s * TILE, TILE)
    smalls = [
        pltpu.make_async_copy(land_ref.at[pl.ds(top_row, HALO)], wet_rows.at[pl.ds(0, HALO)], small_sem.at[0]),
        pltpu.make_async_copy(land_ref.at[pl.ds(own_row, TILE)], wet_rows.at[pl.ds(HALO, TILE)], small_sem.at[1]),
        pltpu.make_async_copy(
            land_ref.at[pl.ds(end_row, HALO)], wet_rows.at[pl.ds(HALO + TILE, HALO)], small_sem.at[2]
        ),
        pltpu.make_async_copy(stations_hbm, stations_ref, small_sem.at[3]),
        pltpu.make_async_copy(observed_hbm, observed_ref, small_sem.at[4]),
        pltpu.make_async_copy(weight_hbm, weight_ref, small_sem.at[5]),
    ]
    load_mean = pltpu.make_async_copy(mean_hbm, mean_in, small_sem.at[6])
    load_mean.start()
    lax.fori_loop(0, CHUNKS, start_load, 0)
    for copy in smalls:
        copy.start()
    load_mean.wait()
    for part in range(2):
        for f in range(6):
            mean_rows[part, pl.ds(HALO * f, HALO)] = mean_in[f, pl.ds(HALO * part, HALO)]
        packed = jnp.concatenate([mean_rows[part, pl.ds(12 * q, 12)] for q in range(4)], axis=1)
        piece_ref[part] = packed
        pieces[core, chip, 1 + part] = packed

    def convert(i):
        for n in range(PER):
            k = i * PER + n
            rows = pl.ds(n * 6 * HALO, 6 * HALO)
            upper = [cov[k, pl.ds(TILE * f, HALO)] for f in range(6)]
            lower = [cov[k, pl.ds(TILE * f + HALO, HALO)] for f in range(6)]
            low[i, rows] = jnp.concatenate(upper, axis=0).astype(jnp.bfloat16)
            high[i, rows] = jnp.concatenate(lower, axis=0).astype(jnp.bfloat16)

    def to_down(i):
        return remote(high.at[i], above.at[i], halo_send.at[0, i], halo_recv.at[0, i], peer(c, down))

    run = y * 8 + zh * 4
    between = (x == 1) | (x == 2)
    next_run = jnp.where(zh == 1, y * 8 + 4, lax.rem(y + 1, 4) * 8)
    last_run = jnp.where(zh == 0, y * 8 + 3, lax.rem(y + 3, 4) * 8 + 7)

    def start_halo(i):
        passed = i < 4
        slot = jnp.minimum(i // 2, 1)
        inner = peer(c, run + 1 + lax.rem(i, 2))

        def one(way, end, direct, source):
            @pl.when(passed & end)
            def _():
                at = relay.at[0, way, slot]
                remote(source.at[i], at, halo_send.at[way, i], relay_recv.at[0, way, slot], inner).start()

            @pl.when(jnp.logical_not(passed & end))
            def _():
                direct(i).start()

        one(0, x == 3, to_down, high)
        one(1, x == 0, to_up, low)

    def relay_far(way, slot):
        return remote(
            relay.at[0, way, slot], relay.at[1, way, slot],
            relay_send.at[0, way, slot], relay_recv.at[1, way, slot], peer(c, far),
        )

    def relay_on(way, slot):
        i = 2 * slot + x - 1
        goal = (above, below)[way].at[i]
        device = peer(c, (next_run, last_run)[way])
        return remote(relay.at[1, way, slot], goal, relay_send.at[1, way, slot], halo_recv.at[way, i], device)

    def pass_far(slot):
        @pl.when(between)
        def _():
            for way in range(2):
                source = (high, low)[way].at[0]
                recv = relay_recv.at[0, way, slot]
                remote(source, relay.at[0, way, slot], halo_send.at[way, 0], recv, peer(c, down)).wait_recv()
                relay_far(way, slot).start()

    def pass_on(slot):
        @pl.when(between)
        def _():
            for way in range(2):
                relay_far(way, slot).wait_recv()
                relay_on(way, slot).start()

    def to_up(i):
        return remote(low.at[i], below.at[i], halo_send.at[1, i], halo_recv.at[1, i], peer(c, up))

    load(0).wait()
    convert(0)
    pl.semaphore_wait(barrier, len(peers))
    shared = []
    for i, q in enumerate([chip] + chips):
        device = same_core(q)
        to = lambda kind: (m_send.at[kind, i], m_recv.at[kind, chip])
        shared.append(remote(piece_ref.at[1], pieces.at[core, chip, 0], *to(0), peer(device, down)))
        shared.append(remote(piece_ref.at[0], pieces.at[core, chip, 3], *to(2), peer(device, up)))
        if i:
            shared.append(remote(piece_ref, pieces.at[core, chip, pl.ds(1, 2)], *to(1), peer(device, s)))
    for copy in shared:
        copy.start()
    start_halo(0)

    def send_halo(i, carry):
        load(i).wait()
        convert(i)

        @pl.when(i < FIRST)
        def _():
            start_halo(i)

        return carry

    lax.fori_loop(1, CHUNKS, send_halo, 0)
    pass_far(0)

    def send_more(i, carry):
        to_down(i - FIRST).wait_send()
        to_up(i - FIRST).wait_send()
        start_halo(i)
        return carry

    lax.fori_loop(FIRST, CHUNKS, send_more, 0)
    pass_far(1)

    lane = lax.broadcasted_iota(jnp.int32, (WIN, WIDTH), 1)
    first, last = lane == 0, lane == WIDTH - 1
    grid_row = s * TILE - HALO + lax.broadcasted_iota(jnp.int32, (WIN, WIDTH), 0)
    inside = ((grid_row >= 0) & (grid_row < NS * TILE)).astype(jnp.float32)
    for copy in smalls:
        copy.wait()
    wet = wet_rows[...].astype(jnp.float32) * inside
    for i, q in enumerate([chip] + chips):
        device = peer(same_core(q), down)
        remote(piece_ref.at[1], pieces.at[core, q, 0], m_send.at[0, 0], m_recv.at[0, q], device).wait_recv()
        remote(piece_ref.at[0], pieces.at[core, q, 3], m_send.at[0, 0], m_recv.at[2, q], device).wait_recv()
        if i:
            theirs = pieces.at[core, q, pl.ds(1, 2)]
            remote(piece_ref, theirs, m_send.at[0, 0], m_recv.at[1, q], device).wait_recv()
    swap = remote(pieces.at[core], pieces.at[core], m_send.at[1, 0], m_recv.at[1, chip], peer(partner, s))
    swap.start()
    swap.wait()
    quarter = lax.broadcasted_iota(jnp.int32, (12, 128), 1) // 32
    for slot in range(4):
        for half in range(2):
            for q in range(4):
                rows = jnp.zeros((12, 128), jnp.float32)
                for p in range(4):
                    value = pieces[p % 2, 2 * half + p // 2, slot]
                    value = pltpu.roll(value, (32 * (p - q)) % 128, 1) if p != q else value
                    rows = jnp.where(quarter == p, value, rows)
                wide[slot, pl.ds(12 * q, 12), 128 * half : 128 * (half + 1)] = rows
    fields = []
    for f in range(6):
        rows = [wide[slot, pl.ds(HALO * f, HALO)] for slot in range(4)]
        fields.append(jnp.concatenate(rows, axis=0) * inside)
    for step in range(STEPS):
        pairs = new_velocities(fields, wet, first, last)
        after = []
        for layer in range(2):
            h = fields[3 * layer]
            depth = (1.0, 2.0)[layer] + h
            u, v = pairs[layer]
            base = 6 * step + 3 * layer
            carried[base] = depth
            carried[base + 1] = u
            carried[base + 2] = v
            h_new = inside * (h - 0.25 * (row_difference(depth * u) + col_difference(depth * v, first, last)))
            after += [h_new, u, v]
        fields = after
    for f in range(6):
        meanf_ref[pl.ds(TILE * f, TILE)] = fields[f][HALO : HALO + TILE]
    surface[pl.ds(NCOL * TILE, TILE)] = (fields[0] + fields[3])[HALO : HALO + TILE]

    def advance(turn, carry):
        i = lax.rem(turn + 4, CHUNKS)
        for at, action, slot in ((ON0, pass_on, 0), (ON1, pass_on, 1)):

            @pl.when(turn == at)
            def _():
                action(slot)

        to_down(i).wait_recv()
        to_up(i).wait_recv()
        for n in range(PER):
            k = i * PER + n
            rows = pl.ds(n * 6 * HALO, 6 * HALO)
            before = above[i, rows].astype(jnp.float32)
            behind = below[i, rows].astype(jnp.float32)
            fields = []
            for f in range(6):
                parts = [
                    before[HALO * f : HALO * (f + 1)],
                    cov[k, pl.ds(TILE * f, TILE)],
                    behind[HALO * f : HALO * (f + 1)],
                ]
                fields.append(jnp.concatenate(parts, axis=0) * inside)
            for step in range(STEPS):
                pairs = new_velocities(fields, wet, first, last)
                after = []
                for layer in range(2):
                    h = fields[3 * layer]
                    u, v = pairs[layer]
                    base = 6 * step + 3 * layer
                    depth = carried[base]
                    rows_flux = depth * u + h * carried[base + 1]
                    cols_flux = depth * v + h * carried[base + 2]
                    change = row_difference(rows_flux) + col_difference(cols_flux, first, last)
                    after += [inside * (h - 0.25 * change), u, v]
                fields = after
            for f in range(6):
                at = pl.ds(pl.multiple_of(k * FR + TILE * f, TILE), TILE)
                for half in range(2):
                    held[half, at] = fields[f][HALO : HALO + TILE, 128 * half : 128 * (half + 1)]
            surface[pl.ds(pl.multiple_of(k * TILE, TILE), TILE)] = (fields[0] + fields[3])[HALO : HALO + TILE]
        return carry

    lax.fori_loop(0, CHUNKS, advance, 0)

    cell = stations_ref[...] - s * (TILE * WIDTH)
    pick = (lax.broadcasted_iota(jnp.int32, (WIDTH, OBS), 0) == cell % WIDTH).astype(jnp.float32)
    at_rows = lax.broadcasted_iota(jnp.int32, (TILE, OBS), 0) == cell // WIDTH
    picked = jnp.dot(surface[...], pick, precision=HIGH, preferred_element_type=jnp.float32)
    picked = picked.reshape(NCOL + 1, TILE, OBS)
    values = jnp.sum(jnp.where(at_rows[None], picked, 0.0), axis=1)
    weight = weight_ref[...]
    mine = values[:NCOL] * weight
    innovation = weight * (observed_ref[...] - values[NCOL:])
    below_first = lax.broadcasted_iota(jnp.int32, (8, OBS), 0) > 0
    sensed[pl.ds(0, NCOL)] = mine
    sensed[pl.ds(NCOL, 8)] = jnp.where(below_first, 0.0, jnp.broadcast_to(innovation, (8, OBS)))
    own_rows = pl.ds(pl.multiple_of(c * NCOL, NCOL), NCOL)
    rows_of = lambda o: pl.ds(pl.multiple_of(o * NCOL, NCOL), NCOL)
    sent = []
    for i, q in enumerate(chips):
        source = sensed.at[pl.ds(0, NCOL)]
        copy = remote(source, right.at[chip, core], send_a.at[i], recv_a.at[chip], peer(same_core(q), s))
        copy.start()
        sent.append(copy)
    right[chip, core] = mine

    def gather_row(fr, carry):
        for half in range(2):
            value = held[half, pl.ds(fr, NCOL, stride=FR)]
            columns[fr, :, 128 * half : 128 * (half + 1)] = value.astype(jnp.bfloat16)
        return carry

    lax.fori_loop(0, FR, gather_row, 0, unroll=8)
    for i, o in enumerate(others):
        source = columns.at[pl.ds(o * PIECE, PIECE)]
        copy = remote(source, cells.at[:, own_rows], send_d.at[i], recv_d.at[c], peer(o, s))
        copy.start()
        sent.append(copy)
    own_cells = pltpu.make_async_copy(columns.at[pl.ds(c * PIECE, PIECE)], cells.at[:, own_rows], own_sem.at[0])
    own_cells.start()

    for q in chips:
        source = sensed.at[pl.ds(0, NCOL)]
        remote(source, right.at[q, core], send_a.at[0], recv_a.at[q], peer(same_core(q), s)).wait_recv()
    swap = remote(right.at[:, core], right.at[:, core], send_a.at[3], recv_a.at[4], peer(partner, s))
    swap.start()
    swap.wait()
    part = lax.dot_general(
        sensed[...],
        right[...].reshape(KALL, OBS),
        (((1,), (1,)), ((), ())),
        precision=HIGH,
        preferred_element_type=jnp.float32,
    )
    block[...] = part
    for i, p in enumerate(planes):
        copy = remote(block, across.at[plane], send_b.at[i], recv_b.at[plane], peer(c, space_of(p)))
        copy.start()
        sent.append(copy)
    across[plane] = part
    for p in planes:
        remote(block, across.at[p], send_b.at[0], recv_b.at[p], peer(c, space_of(p))).wait_recv()
    total = across[0]
    for p in range(1, 16):
        total = total + across[p]
    layers[core, zh, chip] = total
    for i, (q, t, _) in enumerate(line):
        ours = layers.at[core, zh, chip]
        copy = remote(ours, ours, send_c.at[i], recv_c.at[zh, chip], peer(same_core(q), t))
        copy.start()
        sent.append(copy)
    for q, t, side in line:
        theirs = layers.at[core, side, q]
        remote(theirs, theirs, send_c.at[0], recv_c.at[side, q], peer(same_core(q), t)).wait_recv()
    swap = remote(layers.at[core], layers.at[core], send_c.at[7], recv_c.at[2, 0], peer(partner, s))
    swap.start()
    swap.wait()
    for o in range(NC):
        both = [layers[o % 2, side, o // 2, pl.ds(0, NCOL)] for side in range(2)]
        gram[pl.ds(o * NCOL, NCOL)] = both[0] + both[1]
    target = layers[0, 0, 0, pl.ds(NCOL, 8)][:1] + layers[0, 1, 0, pl.ds(NCOL, 8)][:1]
    factor(gram, stack)
    inverse = stack[:, KALL:]
    halfway = jnp.sum(inverse * target, axis=1, keepdims=True)
    weights = jnp.sum(halfway * inverse, axis=0, keepdims=True)
    w_hi = weights.astype(jnp.bfloat16).astype(jnp.float32)
    w_mid = (weights - w_hi).astype(jnp.bfloat16).astype(jnp.float32)
    w_low = weights - w_hi - w_mid
    row16 = lax.broadcasted_iota(jnp.int32, (NCOL, KALL), 0)
    extra = jnp.where(row16 == 0, w_hi, jnp.where(row16 == 1, w_mid, jnp.where(row16 == 2, w_low, 0.0)))
    transform = jnp.concatenate([inverse.astype(jnp.bfloat16), extra.astype(jnp.bfloat16)], axis=0)

    for o in others:
        source = columns.at[pl.ds(0, PIECE)]
        remote(source, cells.at[:, rows_of(o)], send_d.at[0], recv_d.at[o], peer(o, s)).wait_recv()
    own_cells.wait()
    for g in range(GROUPS):
        for fr in range(g * GROUP, (g + 1) * GROUP):
            out = jnp.dot(transform, cells[fr], preferred_element_type=jnp.float32)
            made[fr] = out[:KALL].astype(jnp.bfloat16)
            added[pl.ds(fr, 1)] = out[KALL : KALL + 1] + out[KALL + 1 : KALL + 2] + out[KALL + 2 : KALL + 3]
        some = pl.ds(g * GROUP, GROUP)
        goal = pl.ds(c * PIECE + g * GROUP, GROUP)
        for i, o in enumerate(others):
            copy = remote(
                made.at[some, rows_of(o)], result_ref.at[goal], send_e.at[g, i], recv_e.at[g, c], peer(o, s)
            )
            copy.start()
            sent.append(copy)
    for i, o in enumerate(others):
        copy = remote(added, increment_ref.at[c], send_f.at[i], recv_f.at[c], peer(o, s))
        copy.start()
        sent.append(copy)
    own_made = pltpu.make_async_copy(
        made.at[:, own_rows], result_ref.at[pl.ds(c * PIECE, PIECE)], own_sem.at[0]
    )
    own_made.start()
    increment_ref[c] = added[...]
    for o in others:
        for g in range(GROUPS):
            theirs = result_ref.at[pl.ds(o * PIECE + g * GROUP, GROUP)]
            some = pl.ds(g * GROUP, GROUP)
            remote(made.at[some, own_rows], theirs, send_e.at[0, 0], recv_e.at[g, o], peer(o, s)).wait_recv()
        remote(added, increment_ref.at[o], send_f.at[0], recv_f.at[o], peer(o, s)).wait_recv()
    own_made.wait()
    for copy in sent + shared:
        copy.wait_send()

    def wait_halo(i, carry):
        to_down(i).wait_send()
        to_up(i).wait_send()
        return carry

    lax.fori_loop(CHUNKS - FIRST, CHUNKS, wait_halo, 0)

    @pl.when(between)
    def _():
        for way in range(2):
            for slot in range(2):
                relay_far(way, slot).wait_send()
                relay_on(way, slot).wait_send()


def filter_step(cov, mean, land, stations, observed, weight):
    dma = pltpu.SemaphoreType.DMA
    f32, bf16 = jnp.float32, jnp.bfloat16
    return pl.pallas_call(
        filter_kernel,
        out_shape=(
            jax.ShapeDtypeStruct((FR, NCOL, WIDTH), bf16),
            jax.ShapeDtypeStruct((NC, NCOL, WIDTH), f32),
            jax.ShapeDtypeStruct((FR, WIDTH), f32),
        ),
        in_specs=[HBM] * 6,
        out_specs=(HBM, VMEM, VMEM),
        scratch_shapes=[
            pltpu.VMEM((NCOL, FR, WIDTH), f32),
            pltpu.VMEM((WIN, WIDTH), jnp.int32),
            pltpu.VMEM((1, OBS), jnp.int32),
            pltpu.VMEM((1, OBS), f32),
            pltpu.VMEM((1, OBS), f32),
            pltpu.VMEM((CHUNKS, EDGE, WIDTH), bf16),
            pltpu.VMEM((CHUNKS, EDGE, WIDTH), bf16),
            pltpu.VMEM((CHUNKS, EDGE, WIDTH), bf16),
            pltpu.VMEM((CHUNKS, EDGE, WIDTH), bf16),
            pltpu.VMEM((2, 2, 2, EDGE, WIDTH), bf16),
            pltpu.VMEM((6, TILE, WIDTH // NC), f32),
            pltpu.VMEM((2, 6 * HALO, WIDTH // NC), f32),
            pltpu.VMEM((2, 12, 128), f32),
            pltpu.VMEM((2, 4, 4, 12, 128), f32),
            pltpu.VMEM((4, 6 * HALO, WIDTH), f32),
            pltpu.VMEM((6 * STEPS, WIN, WIDTH), f32),
            pltpu.VMEM((2, NCOL * FR, 128), f32),
            pltpu.VMEM(((NCOL + 1) * TILE, WIDTH), f32),
            pltpu.VMEM((FR, NCOL, WIDTH), bf16),
            pltpu.VMEM((PIECE, KALL, WIDTH), bf16),
            pltpu.VMEM((NCOL + 8, OBS), f32),
            pltpu.VMEM((4, 2, NCOL, OBS), f32),
            pltpu.VMEM((NCOL + 8, KALL), f32),
            pltpu.VMEM((16, NCOL + 8, KALL), f32),
            pltpu.VMEM((2, 2, 4, NCOL + 8, KALL), f32),
            pltpu.VMEM((KALL, KALL), f32),
            pltpu.VMEM((KALL, 2 * KALL), f32),
            pltpu.VMEM((PIECE, KALL, WIDTH), bf16),
            pltpu.VMEM((NCOL, WIDTH), f32),
            dma((CHUNKS,)),
            dma((7,)),
            dma((2, CHUNKS)),
            dma((2, CHUNKS)),
            dma((2, 2, 2)),
            dma((2, 2, 2)),
            dma((3, 4)),
            dma((3, 4)),
            dma((4,)),
            dma((5,)),
            dma((15,)),
            dma((16,)),
            dma((8,)),
            dma((3, 4)),
            dma((NC - 1,)),
            dma((NC,)),
            dma((GROUPS, NC - 1)),
            dma((GROUPS, NC)),
            dma((NC - 1,)),
            dma((NC,)),
            dma((1,)),
        ],
        compiler_params=pltpu.CompilerParams(
            collective_id=0, has_side_effects=True, vmem_limit_bytes=60 * 1024 * 1024
        ),
        name="filter_step",
    )(cov, mean, land, stations, observed, weight)


PARTS = 4
RUN = FR // PARTS


def place_kernel(result_ref, increment_ref, meanf_ref, out_ref, mean_ref, low, held, made, total, in_sem, out_sem):
    def load(q):
        rows = pl.ds(q * RUN, RUN)
        return pltpu.make_async_copy(result_ref.at[rows], low.at[rows], in_sem.at[q])

    def store(q):
        return pltpu.make_async_copy(made.at[q], out_ref.at[:, pl.ds(q * RUN, RUN)], out_sem.at[q])

    for q in range(PARTS):
        load(q).start()
    for q in range(PARTS):
        load(q).wait()
        for half in range(2):
            part = low[pl.ds(q * RUN, RUN), :, 128 * half : 128 * (half + 1)].astype(jnp.float32)
            held[q % 2, half] = part.reshape(RUN * NCOL, 128)
        for j in range(NCOL):
            for half in range(2):
                made[q, j, :, 128 * half : 128 * (half + 1)] = held[q % 2, half, pl.ds(j, RUN, stride=NCOL)]
        store(q).start()
    for o in range(NC):
        rows = pl.ds(o * PIECE, PIECE)
        total[rows] = meanf_ref[rows] + increment_ref[o][:PIECE]
    c = lax.axis_index("cols")
    width = WIDTH // NC
    turned = pltpu.roll(total[...], lax.rem(WIDTH - c * width, WIDTH), 1)
    mean_ref[...] = turned[:, :width]
    for q in range(PARTS):
        store(q).wait()


def place(result, increment, mean_forecast):
    dma = pltpu.SemaphoreType.DMA
    return pl.pallas_call(
        place_kernel,
        out_shape=(
            jax.ShapeDtypeStruct((NCOL, FR, WIDTH), jnp.float32),
            jax.ShapeDtypeStruct((FR, WIDTH // NC), jnp.float32),
        ),
        in_specs=[HBM, VMEM, VMEM],
        out_specs=(HBM, VMEM),
        scratch_shapes=[
            pltpu.VMEM((FR, NCOL, WIDTH), jnp.bfloat16),
            pltpu.VMEM((2, 2, RUN * NCOL, 128), jnp.float32),
            pltpu.VMEM((PARTS, NCOL, RUN, WIDTH), jnp.float32),
            pltpu.VMEM((FR, WIDTH), jnp.float32),
            dma((PARTS,)),
            dma((PARTS,)),
        ],
        compiler_params=pltpu.CompilerParams(vmem_limit_bytes=60 * 1024 * 1024),
        name="place",
    )(result, increment, mean_forecast)


def local(mean_state, covariance, land_mask, stations, observed, obs_weight):
    result, increment, mean_forecast = filter_step(
        covariance.reshape(NCOL, FR, WIDTH), mean_state, land_mask, stations[None], observed[None], obs_weight[None]
    )
    updated, mean = place(result, increment, mean_forecast)
    return mean.reshape(mean_state.shape), updated.reshape(covariance.shape)


def solution(mesh):
    return jax.shard_map(
        local,
        mesh=mesh,
        in_specs=(
            P(None, "space", "cols"),
            P("cols", None, "space", None),
            P(),
            P("space"),
            P("space"),
            P("space"),
        ),
        out_specs=(P(None, "space", "cols"), P("cols", None, "space", None)),
        check_vma=False,
    )
```

```python
import jax
import jax.numpy as jnp
from jax import lax
from jax.experimental import pallas as pl
from jax.experimental.pallas import tpu as pltpu
from jax.sharding import PartitionSpec as P

STEPS = 4
HALO = 8
TILE = 16
WIN = TILE + 2 * HALO
NC = 8
NS = 32
NCOL = 16
KALL = 128
WIDTH = 256
FR = 96
PIECE = 12
OBS = 128

HIGH = lax.Precision.HIGHEST
MESH = pl.DeviceIdType.MESH
ANY = pl.BlockSpec(memory_space=pl.ANY)
VMEM = pl.BlockSpec(memory_space=pltpu.VMEM)
HBM = pl.BlockSpec(memory_space=pltpu.HBM)


def peer(c, s):
    return {"cols": c, "space": s}


def remote(src, dst, send, recv, device):
    return pltpu.make_async_remote_copy(
        src_ref=src, dst_ref=dst, send_sem=send, recv_sem=recv, device_id=device, device_id_type=MESH
    )


def row_difference(a):
    rows = a.shape[0]
    return pltpu.roll(a, rows - 1, 0) - pltpu.roll(a, 1, 0)


def col_difference(a, first, last):
    width = a.shape[1]
    after = jnp.where(last, 0.0, pltpu.roll(a, width - 1, 1))
    before = jnp.where(first, 0.0, pltpu.roll(a, 1, 1))
    return after - before


def new_velocities(fields, wet, first, last):
    top_pressure = fields[0] + fields[3]
    pressures = (top_pressure, top_pressure - 0.125 * fields[0])
    pairs = []
    for layer in range(2):
        u, v = fields[3 * layer + 1], fields[3 * layer + 2]
        p = pressures[layer]
        u_new = wet * (0.975 * u + 0.15 * v - 0.25 * row_difference(p))
        v_new = wet * (0.975 * v - 0.15 * u - 0.25 * col_difference(p, first, last))
        pairs.append((u_new, v_new))
    return pairs


BLOCK = 32


def factor(gram, stack):
    stack[...] = jnp.zeros(stack.shape, jnp.float32)
    row = lax.broadcasted_iota(jnp.int32, (BLOCK, KALL), 0)
    lane = lax.broadcasted_iota(jnp.int32, (BLOCK, KALL), 1)

    def one(b, carry):
        start = pl.multiple_of(b * BLOCK, BLOCK)
        back = lax.rem(KALL - start, KALL)
        done = stack[...]
        turned = pltpu.roll(done[:, :KALL], back, 1)
        product = lax.dot_general(
            turned, done, (((0,), (0,)), ((), ())), precision=HIGH, preferred_element_type=jnp.float32
        )[:BLOCK]
        eye = (lane == row + start).astype(jnp.float32)
        left = gram[pl.ds(start, BLOCK)] + eye - product[:, :KALL]
        right = eye - product[:, KALL:]
        square = pltpu.roll(left, back, 1)
        cols = [jnp.broadcast_to(square[:, m : m + 1], (BLOCK, KALL)) for m in range(BLOCK)]
        scale = jnp.zeros((BLOCK, KALL), jnp.float32)
        for j in range(BLOCK):
            r = lax.rsqrt(cols[j][j : j + 1])
            col = cols[j] * r
            strict = jnp.where(row > j, col, 0.0)
            for m in range(j + 1, BLOCK):
                cols[m] = cols[m] - strict * col[m : m + 1]
            left = left - strict * (left[j : j + 1] * r)
            right = right - strict * (right[j : j + 1] * r)
            scale = jnp.where(row == j, r, scale)
        stack[pl.ds(start, BLOCK), :KALL] = left * scale
        stack[pl.ds(start, BLOCK), KALL:] = right * scale
        return carry

    lax.fori_loop(0, KALL // BLOCK, one, 0)


CHUNKS = 8
FIRST = 8
ON1 = 1
PER = NCOL // CHUNKS
EDGE = PER * 6 * HALO
GROUPS = 4
GROUP = PIECE // GROUPS


def filter_kernel(
    cov_ref, mean_hbm, land_ref, stations_hbm, observed_hbm, weight_hbm,
    result_ref, increment_ref, meanf_ref,
    cov, wet_rows, stations_ref, observed_ref, weight_ref, low, high, above, below, relay, mean_in, mean_rows, piece_ref, pieces, wide, carried, held, surface, columns, cells,
    sensed, right, block, across, layers, gram, stack, made, added,
    load_sem, small_sem, halo_send, halo_recv, relay_send, relay_recv, m_send, m_recv,
    send_a, recv_a, send_b, recv_b, send_c, recv_c, send_d, recv_d, send_e, recv_e, send_f, recv_f, own_sem,
):
    c = lax.axis_index("cols")
    s = lax.axis_index("space")
    down, up = lax.rem(s + 1, NS), lax.rem(s + NS - 1, NS)
    y, zh, x = s // 8, lax.rem(s // 4, 2), lax.rem(s, 4)
    plane = y * 4 + x
    others = [lax.rem(c + i, NC) for i in range(1, NC)]
    planes = [lax.rem(plane + i, 16) for i in range(1, 16)]
    space_of = lambda p: (p // 4) * 8 + zh * 4 + lax.rem(p, 4)
    far = y * 8 + (1 - zh) * 4 + x
    chip, core = c // 2, lax.rem(c, 2)
    partner = 2 * chip + 1 - core
    chips = [lax.rem(chip + i, 4) for i in range(1, 4)]
    line = [(q, s, zh) for q in chips] + [(q, far, 1 - zh) for q in [chip] + chips]
    same_core = lambda q: 2 * q + core

    peers = [peer(same_core(q), t) for t in (down, up) for q in [chip] + chips] + [peer(o, s) for o in others]
    peers += [peer(same_core(q), far) for q in [chip] + chips] + [peer(c, space_of(p)) for p in planes]
    barrier = pltpu.get_barrier_semaphore()
    for device in peers:
        pl.semaphore_signal(barrier, inc=1, device_id=device, device_id_type=MESH)

    def load(i):
        at = pl.ds(pl.multiple_of(i * PER, PER), PER)
        return pltpu.make_async_copy(cov_ref.at[at], cov.at[at], load_sem.at[i])

    def start_load(i, carry):
        load(i).start()
        return carry

    top_row = pl.multiple_of(jnp.maximum(s * TILE - HALO, 0), HALO)
    end_row = pl.multiple_of(jnp.minimum(s * TILE + TILE, NS * TILE - HALO), HALO)
    own_row = pl.multiple_of(s * TILE, TILE)
    smalls = [
        pltpu.make_async_copy(land_ref.at[pl.ds(top_row, HALO)], wet_rows.at[pl.ds(0, HALO)], small_sem.at[0]),
        pltpu.make_async_copy(land_ref.at[pl.ds(own_row, TILE)], wet_rows.at[pl.ds(HALO, TILE)], small_sem.at[1]),
        pltpu.make_async_copy(
            land_ref.at[pl.ds(end_row, HALO)], wet_rows.at[pl.ds(HALO + TILE, HALO)], small_sem.at[2]
        ),
        pltpu.make_async_copy(stations_hbm, stations_ref, small_sem.at[3]),
        pltpu.make_async_copy(observed_hbm, observed_ref, small_sem.at[4]),
        pltpu.make_async_copy(weight_hbm, weight_ref, small_sem.at[5]),
    ]
    load_mean = pltpu.make_async_copy(mean_hbm, mean_in, small_sem.at[6])
    load_mean.start()
    lax.fori_loop(0, CHUNKS, start_load, 0)
    for copy in smalls:
        copy.start()
    load_mean.wait()
    for part in range(2):
        for f in range(6):
            mean_rows[part, pl.ds(HALO * f, HALO)] = mean_in[f, pl.ds(HALO * part, HALO)]
        packed = jnp.concatenate([mean_rows[part, pl.ds(12 * q, 12)] for q in range(4)], axis=1)
        piece_ref[part] = packed
        pieces[core, chip, 1 + part] = packed

    def convert(i):
        for n in range(PER):
            k = i * PER + n
            rows = pl.ds(n * 6 * HALO, 6 * HALO)
            upper = [cov[k, pl.ds(TILE * f, HALO)] for f in range(6)]
            lower = [cov[k, pl.ds(TILE * f + HALO, HALO)] for f in range(6)]
            low[i, rows] = jnp.concatenate(upper, axis=0).astype(jnp.bfloat16)
            high[i, rows] = jnp.concatenate(lower, axis=0).astype(jnp.bfloat16)

    def to_down(i):
        return remote(high.at[i], above.at[i], halo_send.at[0, i], halo_recv.at[0, i], peer(c, down))

    run = y * 8 + zh * 4
    between = (x == 1) | (x == 2)
    next_run = jnp.where(zh == 1, y * 8 + 4, lax.rem(y + 1, 4) * 8)
    last_run = jnp.where(zh == 0, y * 8 + 3, lax.rem(y + 3, 4) * 8 + 7)

    def start_halo(i):
        passed = i < 4
        slot = jnp.minimum(i // 2, 1)
        inner = peer(c, run + 1 + lax.rem(i, 2))

        def one(way, end, direct, source):
            @pl.when(passed & end)
            def _():
                at = relay.at[0, way, slot]
                remote(source.at[i], at, halo_send.at[way, i], relay_recv.at[0, way, slot], inner).start()

            @pl.when(jnp.logical_not(passed & end))
            def _():
                direct(i).start()

        one(0, x == 3, to_down, high)
        one(1, x == 0, to_up, low)

    def relay_far(way, slot):
        return remote(
            relay.at[0, way, slot], relay.at[1, way, slot],
            relay_send.at[0, way, slot], relay_recv.at[1, way, slot], peer(c, far),
        )

    def relay_on(way, slot):
        i = 2 * slot + x - 1
        goal = (above, below)[way].at[i]
        device = peer(c, (next_run, last_run)[way])
        return remote(relay.at[1, way, slot], goal, relay_send.at[1, way, slot], halo_recv.at[way, i], device)

    def pass_far(slot):
        @pl.when(between)
        def _():
            for way in range(2):
                source = (high, low)[way].at[0]
                recv = relay_recv.at[0, way, slot]
                remote(source, relay.at[0, way, slot], halo_send.at[way, 0], recv, peer(c, down)).wait_recv()
                relay_far(way, slot).start()

    def pass_on(slot):
        @pl.when(between)
        def _():
            for way in range(2):
                relay_far(way, slot).wait_recv()
                relay_on(way, slot).start()

    def to_up(i):
        return remote(low.at[i], below.at[i], halo_send.at[1, i], halo_recv.at[1, i], peer(c, up))

    load(0).wait()
    convert(0)
    pl.semaphore_wait(barrier, len(peers))
    shared = []
    for i, q in enumerate([chip] + chips):
        device = same_core(q)
        to = lambda kind: (m_send.at[kind, i], m_recv.at[kind, chip])
        shared.append(remote(piece_ref.at[1], pieces.at[core, chip, 0], *to(0), peer(device, down)))
        shared.append(remote(piece_ref.at[0], pieces.at[core, chip, 3], *to(2), peer(device, up)))
        if i:
            shared.append(remote(piece_ref, pieces.at[core, chip, pl.ds(1, 2)], *to(1), peer(device, s)))
    for copy in shared:
        copy.start()
    start_halo(0)

    def send_halo(i, carry):
        load(i).wait()
        convert(i)

        @pl.when(i < FIRST)
        def _():
            start_halo(i)

        return carry

    lax.fori_loop(1, CHUNKS, send_halo, 0)
    pass_far(0)

    def send_more(i, carry):
        to_down(i - FIRST).wait_send()
        to_up(i - FIRST).wait_send()
        start_halo(i)
        return carry

    lax.fori_loop(FIRST, CHUNKS, send_more, 0)
    pass_far(1)

    lane = lax.broadcasted_iota(jnp.int32, (WIN, WIDTH), 1)
    first, last = lane == 0, lane == WIDTH - 1
    grid_row = s * TILE - HALO + lax.broadcasted_iota(jnp.int32, (WIN, WIDTH), 0)
    inside = ((grid_row >= 0) & (grid_row < NS * TILE)).astype(jnp.float32)
    for copy in smalls:
        copy.wait()
    wet = wet_rows[...].astype(jnp.float32) * inside
    for i, q in enumerate([chip] + chips):
        device = peer(same_core(q), down)
        remote(piece_ref.at[1], pieces.at[core, q, 0], m_send.at[0, 0], m_recv.at[0, q], device).wait_recv()
        remote(piece_ref.at[0], pieces.at[core, q, 3], m_send.at[0, 0], m_recv.at[2, q], device).wait_recv()
        if i:
            theirs = pieces.at[core, q, pl.ds(1, 2)]
            remote(piece_ref, theirs, m_send.at[0, 0], m_recv.at[1, q], device).wait_recv()
    swap = remote(pieces.at[core], pieces.at[core], m_send.at[1, 0], m_recv.at[1, chip], peer(partner, s))
    swap.start()
    swap.wait()
    pass_on(0)
    quarter = lax.broadcasted_iota(jnp.int32, (12, 128), 1) // 32
    for slot in range(4):
        for half in range(2):
            for q in range(4):
                rows = jnp.zeros((12, 128), jnp.float32)
                for p in range(4):
                    value = pieces[p % 2, 2 * half + p // 2, slot]
                    value = pltpu.roll(value, (32 * (p - q)) % 128, 1) if p != q else value
                    rows = jnp.where(quarter == p, value, rows)
                wide[slot, pl.ds(12 * q, 12), 128 * half : 128 * (half + 1)] = rows
    fields = []
    for f in range(6):
        rows = [wide[slot, pl.ds(HALO * f, HALO)] for slot in range(4)]
        fields.append(jnp.concatenate(rows, axis=0) * inside)
    for step in range(STEPS):
        pairs = new_velocities(fields, wet, first, last)
        after = []
        for layer in range(2):
            h = fields[3 * layer]
            depth = (1.0, 2.0)[layer] + h
            u, v = pairs[layer]
            base = 6 * step + 3 * layer
            carried[base] = depth
            carried[base + 1] = u
            carried[base + 2] = v
            h_new = inside * (h - 0.25 * (row_difference(depth * u) + col_difference(depth * v, first, last)))
            after += [h_new, u, v]
        fields = after
    for f in range(6):
        meanf_ref[pl.ds(TILE * f, TILE)] = fields[f][HALO : HALO + TILE]
    surface[pl.ds(NCOL * TILE, TILE)] = (fields[0] + fields[3])[HALO : HALO + TILE]

    def advance(turn, carry):
        i = lax.rem(turn + 4, CHUNKS)
        for at, action, slot in ((ON1, pass_on, 1),):

            @pl.when(turn == at)
            def _():
                action(slot)

        to_down(i).wait_recv()
        to_up(i).wait_recv()
        for n in range(PER):
            k = i * PER + n
            rows = pl.ds(n * 6 * HALO, 6 * HALO)
            before = above[i, rows].astype(jnp.float32)
            behind = below[i, rows].astype(jnp.float32)
            fields = []
            for f in range(6):
                parts = [
                    before[HALO * f : HALO * (f + 1)],
                    cov[k, pl.ds(TILE * f, TILE)],
                    behind[HALO * f : HALO * (f + 1)],
                ]
                fields.append(jnp.concatenate(parts, axis=0) * inside)
            for step in range(STEPS):
                pairs = new_velocities(fields, wet, first, last)
                after = []
                for layer in range(2):
                    h = fields[3 * layer]
                    u, v = pairs[layer]
                    base = 6 * step + 3 * layer
                    depth = carried[base]
                    rows_flux = depth * u + h * carried[base + 1]
                    cols_flux = depth * v + h * carried[base + 2]
                    change = row_difference(rows_flux) + col_difference(cols_flux, first, last)
                    after += [inside * (h - 0.25 * change), u, v]
                fields = after
            for f in range(6):
                at = pl.ds(pl.multiple_of(k * FR + TILE * f, TILE), TILE)
                for half in range(2):
                    held[half, at] = fields[f][HALO : HALO + TILE, 128 * half : 128 * (half + 1)]
            surface[pl.ds(pl.multiple_of(k * TILE, TILE), TILE)] = (fields[0] + fields[3])[HALO : HALO + TILE]
        return carry

    lax.fori_loop(0, CHUNKS, advance, 0)

    cell = stations_ref[...] - s * (TILE * WIDTH)
    pick = (lax.broadcasted_iota(jnp.int32, (WIDTH, OBS), 0) == cell % WIDTH).astype(jnp.float32)
    at_rows = lax.broadcasted_iota(jnp.int32, (TILE, OBS), 0) == cell // WIDTH
    picked = jnp.dot(surface[...], pick, precision=HIGH, preferred_element_type=jnp.float32)
    picked = picked.reshape(NCOL + 1, TILE, OBS)
    values = jnp.sum(jnp.where(at_rows[None], picked, 0.0), axis=1)
    weight = weight_ref[...]
    mine = values[:NCOL] * weight
    innovation = weight * (observed_ref[...] - values[NCOL:])
    below_first = lax.broadcasted_iota(jnp.int32, (8, OBS), 0) > 0
    sensed[pl.ds(0, NCOL)] = mine
    sensed[pl.ds(NCOL, 8)] = jnp.where(below_first, 0.0, jnp.broadcast_to(innovation, (8, OBS)))
    own_rows = pl.ds(pl.multiple_of(c * NCOL, NCOL), NCOL)
    rows_of = lambda o: pl.ds(pl.multiple_of(o * NCOL, NCOL), NCOL)
    sent = []
    for i, q in enumerate(chips):
        source = sensed.at[pl.ds(0, NCOL)]
        copy = remote(source, right.at[chip, core], send_a.at[i], recv_a.at[chip], peer(same_core(q), s))
        copy.start()
        sent.append(copy)
    right[chip, core] = mine

    def gather_row(fr, carry):
        for half in range(2):
            value = held[half, pl.ds(fr, NCOL, stride=FR)]
            columns[fr, :, 128 * half : 128 * (half + 1)] = value.astype(jnp.bfloat16)
        return carry

    lax.fori_loop(0, FR, gather_row, 0, unroll=8)
    for i, o in enumerate(others):
        source = columns.at[pl.ds(o * PIECE, PIECE)]
        copy = remote(source, cells.at[:, own_rows], send_d.at[i], recv_d.at[c], peer(o, s))
        copy.start()
        sent.append(copy)
    own_cells = pltpu.make_async_copy(columns.at[pl.ds(c * PIECE, PIECE)], cells.at[:, own_rows], own_sem.at[0])
    own_cells.start()

    for q in chips:
        source = sensed.at[pl.ds(0, NCOL)]
        remote(source, right.at[q, core], send_a.at[0], recv_a.at[q], peer(same_core(q), s)).wait_recv()
    swap = remote(right.at[:, core], right.at[:, core], send_a.at[3], recv_a.at[4], peer(partner, s))
    swap.start()
    swap.wait()
    part = lax.dot_general(
        sensed[...],
        right[...].reshape(KALL, OBS),
        (((1,), (1,)), ((), ())),
        precision=HIGH,
        preferred_element_type=jnp.float32,
    )
    block[...] = part
    for i, p in enumerate(planes):
        copy = remote(block, across.at[plane], send_b.at[i], recv_b.at[plane], peer(c, space_of(p)))
        copy.start()
        sent.append(copy)
    across[plane] = part
    for p in planes:
        remote(block, across.at[p], send_b.at[0], recv_b.at[p], peer(c, space_of(p))).wait_recv()
    total = across[0]
    for p in range(1, 16):
        total = total + across[p]
    layers[core, zh, chip] = total
    for i, (q, t, _) in enumerate(line):
        ours = layers.at[core, zh, chip]
        copy = remote(ours, ours, send_c.at[i], recv_c.at[zh, chip], peer(same_core(q), t))
        copy.start()
        sent.append(copy)
    for q, t, side in line:
        theirs = layers.at[core, side, q]
        remote(theirs, theirs, send_c.at[0], recv_c.at[side, q], peer(same_core(q), t)).wait_recv()
    swap = remote(layers.at[core], layers.at[core], send_c.at[7], recv_c.at[2, 0], peer(partner, s))
    swap.start()
    swap.wait()
    for o in range(NC):
        both = [layers[o % 2, side, o // 2, pl.ds(0, NCOL)] for side in range(2)]
        gram[pl.ds(o * NCOL, NCOL)] = both[0] + both[1]
    target = layers[0, 0, 0, pl.ds(NCOL, 8)][:1] + layers[0, 1, 0, pl.ds(NCOL, 8)][:1]
    factor(gram, stack)
    inverse = stack[:, KALL:]
    halfway = jnp.sum(inverse * target, axis=1, keepdims=True)
    weights = jnp.sum(halfway * inverse, axis=0, keepdims=True)
    w_hi = weights.astype(jnp.bfloat16).astype(jnp.float32)
    w_mid = (weights - w_hi).astype(jnp.bfloat16).astype(jnp.float32)
    w_low = weights - w_hi - w_mid
    row16 = lax.broadcasted_iota(jnp.int32, (NCOL, KALL), 0)
    extra = jnp.where(row16 == 0, w_hi, jnp.where(row16 == 1, w_mid, jnp.where(row16 == 2, w_low, 0.0)))
    transform = jnp.concatenate([inverse.astype(jnp.bfloat16), extra.astype(jnp.bfloat16)], axis=0)

    for o in others:
        source = columns.at[pl.ds(0, PIECE)]
        remote(source, cells.at[:, rows_of(o)], send_d.at[0], recv_d.at[o], peer(o, s)).wait_recv()
    own_cells.wait()
    for g in range(GROUPS):
        for fr in range(g * GROUP, (g + 1) * GROUP):
            out = jnp.dot(transform, cells[fr], preferred_element_type=jnp.float32)
            made[fr] = out[:KALL].astype(jnp.bfloat16)
            added[pl.ds(fr, 1)] = out[KALL : KALL + 1] + out[KALL + 1 : KALL + 2] + out[KALL + 2 : KALL + 3]
        some = pl.ds(g * GROUP, GROUP)
        goal = pl.ds(c * PIECE + g * GROUP, GROUP)
        for i, o in enumerate(others):
            copy = remote(
                made.at[some, rows_of(o)], result_ref.at[goal], send_e.at[g, i], recv_e.at[g, c], peer(o, s)
            )
            copy.start()
            sent.append(copy)
    for i, o in enumerate(others):
        copy = remote(added, increment_ref.at[c], send_f.at[i], recv_f.at[c], peer(o, s))
        copy.start()
        sent.append(copy)
    own_made = pltpu.make_async_copy(
        made.at[:, own_rows], result_ref.at[pl.ds(c * PIECE, PIECE)], own_sem.at[0]
    )
    own_made.start()
    increment_ref[c] = added[...]
    for o in others:
        for g in range(GROUPS):
            theirs = result_ref.at[pl.ds(o * PIECE + g * GROUP, GROUP)]
            some = pl.ds(g * GROUP, GROUP)
            remote(made.at[some, own_rows], theirs, send_e.at[0, 0], recv_e.at[g, o], peer(o, s)).wait_recv()
        remote(added, increment_ref.at[o], send_f.at[0], recv_f.at[o], peer(o, s)).wait_recv()
    own_made.wait()
    for copy in sent + shared:
        copy.wait_send()

    def wait_halo(i, carry):
        to_down(i).wait_send()
        to_up(i).wait_send()
        return carry

    lax.fori_loop(CHUNKS - FIRST, CHUNKS, wait_halo, 0)

    @pl.when(between)
    def _():
        for way in range(2):
            for slot in range(2):
                relay_far(way, slot).wait_send()
                relay_on(way, slot).wait_send()


def filter_step(cov, mean, land, stations, observed, weight):
    dma = pltpu.SemaphoreType.DMA
    f32, bf16 = jnp.float32, jnp.bfloat16
    return pl.pallas_call(
        filter_kernel,
        out_shape=(
            jax.ShapeDtypeStruct((FR, NCOL, WIDTH), bf16),
            jax.ShapeDtypeStruct((NC, NCOL, WIDTH), f32),
            jax.ShapeDtypeStruct((FR, WIDTH), f32),
        ),
        in_specs=[HBM] * 6,
        out_specs=(HBM, VMEM, VMEM),
        scratch_shapes=[
            pltpu.VMEM((NCOL, FR, WIDTH), f32),
            pltpu.VMEM((WIN, WIDTH), jnp.int32),
            pltpu.VMEM((1, OBS), jnp.int32),
            pltpu.VMEM((1, OBS), f32),
            pltpu.VMEM((1, OBS), f32),
            pltpu.VMEM((CHUNKS, EDGE, WIDTH), bf16),
            pltpu.VMEM((CHUNKS, EDGE, WIDTH), bf16),
            pltpu.VMEM((CHUNKS, EDGE, WIDTH), bf16),
            pltpu.VMEM((CHUNKS, EDGE, WIDTH), bf16),
            pltpu.VMEM((2, 2, 2, EDGE, WIDTH), bf16),
            pltpu.VMEM((6, TILE, WIDTH // NC), f32),
            pltpu.VMEM((2, 6 * HALO, WIDTH // NC), f32),
            pltpu.VMEM((2, 12, 128), f32),
            pltpu.VMEM((2, 4, 4, 12, 128), f32),
            pltpu.VMEM((4, 6 * HALO, WIDTH), f32),
            pltpu.VMEM((6 * STEPS, WIN, WIDTH), f32),
            pltpu.VMEM((2, NCOL * FR, 128), f32),
            pltpu.VMEM(((NCOL + 1) * TILE, WIDTH), f32),
            pltpu.VMEM((FR, NCOL, WIDTH), bf16),
            pltpu.VMEM((PIECE, KALL, WIDTH), bf16),
            pltpu.VMEM((NCOL + 8, OBS), f32),
            pltpu.VMEM((4, 2, NCOL, OBS), f32),
            pltpu.VMEM((NCOL + 8, KALL), f32),
            pltpu.VMEM((16, NCOL + 8, KALL), f32),
            pltpu.VMEM((2, 2, 4, NCOL + 8, KALL), f32),
            pltpu.VMEM((KALL, KALL), f32),
            pltpu.VMEM((KALL, 2 * KALL), f32),
            pltpu.VMEM((PIECE, KALL, WIDTH), bf16),
            pltpu.VMEM((NCOL, WIDTH), f32),
            dma((CHUNKS,)),
            dma((7,)),
            dma((2, CHUNKS)),
            dma((2, CHUNKS)),
            dma((2, 2, 2)),
            dma((2, 2, 2)),
            dma((3, 4)),
            dma((3, 4)),
            dma((4,)),
            dma((5,)),
            dma((15,)),
            dma((16,)),
            dma((8,)),
            dma((3, 4)),
            dma((NC - 1,)),
            dma((NC,)),
            dma((GROUPS, NC - 1)),
            dma((GROUPS, NC)),
            dma((NC - 1,)),
            dma((NC,)),
            dma((1,)),
        ],
        compiler_params=pltpu.CompilerParams(
            collective_id=0, has_side_effects=True, vmem_limit_bytes=60 * 1024 * 1024
        ),
        name="filter_step",
    )(cov, mean, land, stations, observed, weight)


PARTS = 4
RUN = FR // PARTS


def place_kernel(result_ref, increment_ref, meanf_ref, out_ref, mean_ref, low, held, made, total, in_sem, out_sem):
    def load(q):
        rows = pl.ds(q * RUN, RUN)
        return pltpu.make_async_copy(result_ref.at[rows], low.at[rows], in_sem.at[q])

    def store(q):
        return pltpu.make_async_copy(made.at[q], out_ref.at[:, pl.ds(q * RUN, RUN)], out_sem.at[q])

    for q in range(PARTS):
        load(q).start()
    for q in range(PARTS):
        load(q).wait()
        for half in range(2):
            part = low[pl.ds(q * RUN, RUN), :, 128 * half : 128 * (half + 1)].astype(jnp.float32)
            held[q % 2, half] = part.reshape(RUN * NCOL, 128)
        for j in range(NCOL):
            for half in range(2):
                made[q, j, :, 128 * half : 128 * (half + 1)] = held[q % 2, half, pl.ds(j, RUN, stride=NCOL)]
        store(q).start()
    for o in range(NC):
        rows = pl.ds(o * PIECE, PIECE)
        total[rows] = meanf_ref[rows] + increment_ref[o][:PIECE]
    c = lax.axis_index("cols")
    width = WIDTH // NC
    turned = pltpu.roll(total[...], lax.rem(WIDTH - c * width, WIDTH), 1)
    mean_ref[...] = turned[:, :width]
    for q in range(PARTS):
        store(q).wait()


def place(result, increment, mean_forecast):
    dma = pltpu.SemaphoreType.DMA
    return pl.pallas_call(
        place_kernel,
        out_shape=(
            jax.ShapeDtypeStruct((NCOL, FR, WIDTH), jnp.float32),
            jax.ShapeDtypeStruct((FR, WIDTH // NC), jnp.float32),
        ),
        in_specs=[HBM, VMEM, VMEM],
        out_specs=(HBM, VMEM),
        scratch_shapes=[
            pltpu.VMEM((FR, NCOL, WIDTH), jnp.bfloat16),
            pltpu.VMEM((2, 2, RUN * NCOL, 128), jnp.float32),
            pltpu.VMEM((PARTS, NCOL, RUN, WIDTH), jnp.float32),
            pltpu.VMEM((FR, WIDTH), jnp.float32),
            dma((PARTS,)),
            dma((PARTS,)),
        ],
        compiler_params=pltpu.CompilerParams(vmem_limit_bytes=60 * 1024 * 1024),
        name="place",
    )(result, increment, mean_forecast)


def local(mean_state, covariance, land_mask, stations, observed, obs_weight):
    result, increment, mean_forecast = filter_step(
        covariance.reshape(NCOL, FR, WIDTH), mean_state, land_mask, stations[None], observed[None], obs_weight[None]
    )
    updated, mean = place(result, increment, mean_forecast)
    return mean.reshape(mean_state.shape), updated.reshape(covariance.shape)


def solution(mesh):
    return jax.shard_map(
        local,
        mesh=mesh,
        in_specs=(
            P(None, "space", "cols"),
            P("cols", None, "space", None),
            P(),
            P("space"),
            P("space"),
            P("space"),
        ),
        out_specs=(P(None, "space", "cols"), P("cols", None, "space", None)),
        check_vma=False,
    )
```
